32 devices in a mesh: row: 32 (over z, y, x, core), col: 1.
Axes of the slice: x: 2, y: 2, z: 4, core: 2. Of those that a mesh axis runs over, the one named last changes fastest.
Arguments:
- convolution_input: bfloat16 [256, 256, 128], P('row', 'col'), may hold values from -6 to 6
- pair: bfloat16 [256, 256, 128], P('row', 'col'), may hold values from -6 to 6
- out_cot: bfloat16 [256, 256, 128], P('row', 'col'), may hold values from -6 to 6
- tile_mask: int32 [2, 2], replicated, may hold values 0 or 1
- dilation: int32 [128], replicated, may hold values from 1 to 4, as said below
- norm_in_gain: float32 [128], replicated, may hold values from 0.5 to 1.5
- norm_in_bias: float32 [128], replicated, may hold values from -3 to 3
- proj_weight: bfloat16 [128, 256], replicated, may hold values from -0.5 to 0.5
- gate_weight: bfloat16 [128, 256], replicated, may hold values from -0.5 to 0.5
- norm_out_gain: float32 [128], replicated, may hold values from 0.5 to 1.5
- norm_out_bias: float32 [128], replicated, may hold values from -3 to 3
- out_weight: bfloat16 [128, 128], replicated, may hold values from -0.5 to 0.5
- out_gate_weight: bfloat16 [128, 128], replicated, may hold values from -0.5 to 0.5
- conv_weight: bfloat16 [9, 128, 128], replicated, may hold values from -0.1875 to 0.1875
Outputs:
- input_grad: bfloat16 [256, 256, 128], P('row', 'col')
- conv_weight_grad: float32 [9, 128, 128], replicated
The draws below stay inside these ranges and needn't reach their ends.
Inputs may be any that keep to these rules, and one draw needn't show every extreme that they name: Some channel has dilation 4.
All inputs are finite; a program needn't handle non-finite values.
Results may differ from the reference program's by a relative error of at most 0.0065.
Values may be sent and summed in bfloat16 or wider, within the bound.
A program may use at most 64 MiB of HBM per device.

```python
import jax
import jax.numpy as jnp
from jax import lax

PAIR_CHANNELS = 128
TILE = 128
DILATION_LIMIT = 4
N = 256
TILES = 2


def draw_dilation(key, part):
    key = jax.random.fold_in(key, 7)
    key_entries, key_spot = jax.random.split(key)
    value_entries = jax.random.randint(key_entries, (PAIR_CHANNELS,), 1, DILATION_LIMIT + 1, dtype=jnp.int32)
    tap_position = jax.random.randint(key_spot, (), 0, PAIR_CHANNELS, dtype=jnp.int32)
    return value_entries.at[tap_position].set(DILATION_LIMIT)


def with_ends(values, key, low, largest):
    extent = values.shape
    place = [jax.random.randint(jax.random.fold_in(key, axis), (), 0, extent[axis]) for axis in range(len(extent))]
    values = values.at[tuple(place)].set(low)
    longest = extent.index(max(extent))
    place[longest] = (place[longest] + 1) % extent[longest]
    return values.at[tuple(place)].set(largest)


def block_scale(rng, extent, shards, smallest, top_value):
    loudness = 1.0
    for position, shards_of in shards:
        heights = jax.random.uniform(jax.random.fold_in(jax.random.fold_in(rng, 6), position), (shards_of,), jnp.float32, smallest / len(shards), top_value / len(shards))
        loudness = loudness * jnp.repeat(jnp.exp(heights), extent[position] // shards_of).reshape((-1,) + (1,) * (len(extent) - 1 - position))
    return loudness


def scatter_about(stream_key, extent, width, limit, shards=(), kind=jnp.bfloat16):
    result = width * jax.random.normal(stream_key, extent, jnp.float32)
    if shards:
        result = result * block_scale(stream_key, extent, shards, -0.22, 0.18)
    return jnp.clip(result, -limit, limit).astype(kind)


def setup_inputs(seed: int = 0) -> dict:
    arg_keys = jax.random.split(jax.random.key(seed), 15)
    convolution_input = scatter_about(arg_keys[0], (N, N, PAIR_CHANNELS), 1.0, 6.0, ((0, 32),))
    pair = scatter_about(arg_keys[1], (N, N, PAIR_CHANNELS), 1.0, 6.0, ((0, 32),))
    out_cot = scatter_about(arg_keys[2], (N, N, PAIR_CHANNELS), 1.0, 6.0, ((0, 32),))
    tile_mask = with_ends((jax.random.randint(arg_keys[3], (TILES, TILES), 0, 2) < 1).astype(jnp.int32), jax.random.fold_in(arg_keys[3], 1), 0, 1)
    dilation = draw_dilation(jax.random.fold_in(arg_keys[14], 71), 0)
    norm_in_gain = jnp.clip(1.0 + 0.1 * jax.random.normal(arg_keys[5], (PAIR_CHANNELS,), jnp.float32), 0.5, 1.5)
    norm_in_bias = scatter_about(arg_keys[6], (PAIR_CHANNELS,), 0.5, 3.0, (), jnp.float32)
    proj_weight = scatter_about(arg_keys[7], (PAIR_CHANNELS, 2 * PAIR_CHANNELS), PAIR_CHANNELS ** -0.5, 0.5)
    gate_weight = scatter_about(arg_keys[8], (PAIR_CHANNELS, 2 * PAIR_CHANNELS), PAIR_CHANNELS ** -0.5, 0.5)
    norm_out_gain = jnp.clip(1.0 + 0.1 * jax.random.normal(arg_keys[9], (PAIR_CHANNELS,), jnp.float32), 0.5, 1.5)
    norm_out_bias = scatter_about(arg_keys[10], (PAIR_CHANNELS,), 0.5, 3.0, (), jnp.float32)
    out_weight = scatter_about(arg_keys[11], (PAIR_CHANNELS, PAIR_CHANNELS), PAIR_CHANNELS ** -0.5, 0.5)
    out_gate_weight = scatter_about(arg_keys[12], (PAIR_CHANNELS, PAIR_CHANNELS), PAIR_CHANNELS ** -0.5, 0.5)
    conv_weight = scatter_about(arg_keys[13], (9, PAIR_CHANNELS, PAIR_CHANNELS), (9 * PAIR_CHANNELS) ** -0.5, 0.1875)
    return dict(convolution_input=convolution_input, pair=pair, out_cot=out_cot, tile_mask=tile_mask, dilation=dilation, norm_in_gain=norm_in_gain, norm_in_bias=norm_in_bias, proj_weight=proj_weight, gate_weight=gate_weight, norm_out_gain=norm_out_gain, norm_out_bias=norm_out_bias, out_weight=out_weight, out_gate_weight=out_gate_weight, conv_weight=conv_weight)


EPSILON = 1e-05

def layer_norm(value_entries, scale_gain, shift_bias, channel_axis):
    mean_value = lax.optimization_barrier(jnp.mean(value_entries, axis=channel_axis, keepdims=True))
    centred = value_entries - mean_value
    variance = lax.optimization_barrier(jnp.mean(centred * centred, axis=channel_axis, keepdims=True))
    inv_deviation = lax.rsqrt(variance + EPSILON)
    normed = centred * inv_deviation
    return (normed * scale_gain + shift_bias, normed, inv_deviation)

def norm_back(incoming, normed, inv_deviation, scale_gain, channel_axis):
    scaled = incoming * scale_gain
    mean_first = lax.optimization_barrier(jnp.mean(scaled, axis=channel_axis, keepdims=True))
    second = lax.optimization_barrier(jnp.mean(scaled * normed, axis=channel_axis, keepdims=True))
    return inv_deviation * (scaled - mean_first - normed * second)

def offsets():
    return [(row_stride, column_stride) for row_stride in (-1, 0, 1) for column_stride in (-1, 0, 1)]

def channel_product(pieces):
    return jnp.dot(pieces[0], pieces[1].T, preferred_element_type=jnp.float32).astype(jnp.bfloat16)

def channel_back(pieces):
    incoming, left_side, right_side = pieces
    grad_left = jnp.dot(incoming, right_side, preferred_element_type=jnp.float32)
    grad_right = jnp.dot(incoming.T, left_side, preferred_element_type=jnp.float32)
    return (grad_left, grad_right)

def reference(convolution_input, pair, out_cot, tile_mask, dilation, norm_in_gain, norm_in_bias, proj_weight, gate_weight, norm_out_gain, norm_out_bias, out_weight, out_gate_weight, conv_weight):
    pair_mask = jnp.repeat(jnp.repeat(tile_mask.astype(jnp.float32), TILE, 0), TILE, 1)
    normed_in, in_hat, in_inv = layer_norm(pair.astype(jnp.float32), norm_in_gain, norm_in_bias, 2)
    pair_norm = normed_in.astype(jnp.bfloat16)
    norm_wide = pair_norm.astype(jnp.float32)
    projected = jnp.einsum('ijc,ce->ije', norm_wide, proj_weight.astype(jnp.float32))
    gate_lin = jnp.einsum('ijc,ce->ije', norm_wide, gate_weight.astype(jnp.float32))
    gate_sig = jax.nn.sigmoid(gate_lin)
    both_sides = (projected * gate_sig * pair_mask[:, :, None]).astype(jnp.bfloat16)
    left_side = jnp.moveaxis(both_sides[:, :, :PAIR_CHANNELS], 2, 0)
    right_side = jnp.moveaxis(both_sides[:, :, PAIR_CHANNELS:], 2, 0)
    product = jnp.moveaxis(lax.map(channel_product, (left_side, right_side)), 0, 2)
    normed_out, out_hat, out_inv = layer_norm(product.astype(jnp.float32), norm_out_gain, norm_out_bias, 2)
    product_norm = normed_out.astype(jnp.bfloat16)
    out_lin = jnp.einsum('ijc,cd->ijd', product_norm.astype(jnp.float32), out_weight.astype(jnp.float32))
    out_gate = jax.nn.sigmoid(jnp.einsum('ijc,cd->ijd', norm_wide, out_gate_weight.astype(jnp.float32)))
    cotangent = out_cot.astype(jnp.float32)
    grad_lin = (cotangent * out_gate).astype(jnp.bfloat16)
    grad_gate = (cotangent * out_lin * out_gate * (1.0 - out_gate)).astype(jnp.bfloat16)
    grad_norm = jnp.einsum('ijd,cd->ijc', grad_lin.astype(jnp.float32), out_weight.astype(jnp.float32))
    grad_product = norm_back(grad_norm, out_hat, out_inv, norm_out_gain, 2).astype(jnp.bfloat16)
    grad_left, grad_right = lax.map(channel_back, (jnp.moveaxis(grad_product, 2, 0), left_side, right_side))
    grad_both = jnp.concatenate([jnp.moveaxis(grad_left, 0, 2), jnp.moveaxis(grad_right, 0, 2)], axis=2)
    grad_sides = (grad_both * pair_mask[:, :, None]).astype(jnp.bfloat16).astype(jnp.float32)
    grad_proj = (grad_sides * gate_sig).astype(jnp.bfloat16)
    grad_gatelin = (grad_sides * projected * gate_sig * (1.0 - gate_sig)).astype(jnp.bfloat16)
    grad_in = jnp.einsum('ije,ce->ijc', grad_proj.astype(jnp.float32), proj_weight.astype(jnp.float32))
    grad_in = grad_in + jnp.einsum('ije,ce->ijc', grad_gatelin.astype(jnp.float32), gate_weight.astype(jnp.float32))
    grad_in = grad_in + jnp.einsum('ijd,cd->ijc', grad_gate.astype(jnp.float32), out_gate_weight.astype(jnp.float32))
    pair_gradient = (cotangent + norm_back(grad_in, in_hat, in_inv, norm_in_gain, 2)).astype(jnp.bfloat16)
    border_margin = ((DILATION_LIMIT, DILATION_LIMIT), (DILATION_LIMIT, DILATION_LIMIT), (0, 0))
    bordered_gradient = jnp.pad(pair_gradient, border_margin)
    bordered_input = jnp.pad(convolution_input, border_margin)
    selected_entries = [dilation == shift_amount for shift_amount in range(1, DILATION_LIMIT + 1)]
    back_sum = pair_gradient.astype(jnp.float32)
    weight_terms = []
    for tap_index, (row_stride, column_stride) in enumerate(offsets()):
        tap_image = jnp.einsum('pqo,io->pqi', bordered_gradient.astype(jnp.float32), conv_weight[tap_index].astype(jnp.float32))
        contribution = jnp.zeros(back_sum.shape, jnp.float32)
        shifted_input = jnp.zeros_like(convolution_input)
        for shift_amount in range(1, DILATION_LIMIT + 1):
            row_source = DILATION_LIMIT - shift_amount * row_stride
            column_source = DILATION_LIMIT - shift_amount * column_stride
            contribution = jnp.where(selected_entries[shift_amount - 1], tap_image[row_source:row_source + N, column_source:column_source + N], contribution)
            row_inside = DILATION_LIMIT + shift_amount * row_stride
            column_inside = DILATION_LIMIT + shift_amount * column_stride
            shifted_input = jnp.where(selected_entries[shift_amount - 1], bordered_input[row_inside:row_inside + N, column_inside:column_inside + N], shifted_input)
        back_sum = back_sum + contribution
        weight_terms.append(jnp.einsum('pqi,pqo->io', shifted_input.astype(jnp.float32), pair_gradient.astype(jnp.float32)))
    input_grad = back_sum.astype(jnp.bfloat16)
    conv_weight_grad = jnp.stack(weight_terms) / N
    return (input_grad, conv_weight_grad)
```

```python
import functools

import jax
import jax.numpy as jnp
from jax import lax
from jax.experimental import pallas as pl
from jax.experimental.pallas import tpu as pltpu
from jax.sharding import PartitionSpec as P

DILATION_LIMIT = 4


EPSILON = 1e-05


def extended(block, sides, width):
    for axis, dim in sides:
        count = lax.axis_size(axis)
        forward = [(i, i + 1) for i in range(count - 1)]
        backward = [(target, source) for source, target in forward]
        low = lax.ppermute(
            lax.slice_in_dim(block, block.shape[dim] - width, None, axis=dim), axis, forward
        )
        high = lax.ppermute(lax.slice_in_dim(block, 0, width, axis=dim), axis, backward)
        block = jnp.concatenate([low, block, high], axis=dim)
    return block


def layer_norm(value_entries, scale_gain, shift_bias, channel_axis):
    mean_value = jnp.mean(value_entries, axis=channel_axis, keepdims=True)
    centred = value_entries - mean_value
    variance = jnp.mean(centred * centred, axis=channel_axis, keepdims=True)
    inv_deviation = lax.rsqrt(variance + EPSILON)
    normed = centred * inv_deviation
    return (normed * scale_gain + shift_bias, normed, inv_deviation)


def norm_back(incoming, normed, inv_deviation, scale_gain, channel_axis):
    scaled = incoming * scale_gain
    mean_first = jnp.mean(scaled, axis=channel_axis, keepdims=True)
    second = jnp.mean(scaled * normed, axis=channel_axis, keepdims=True)
    return inv_deviation * (scaled - mean_first - normed * second)


def offsets():
    return [
        (row_stride, column_stride) for row_stride in (-1, 0, 1) for column_stride in (-1, 0, 1)
    ]


def tap_weights(conv_weight, dilation):
    by_tap = jnp.swapaxes(conv_weight, 1, 2)
    blocks = []
    for amount in range(1, DILATION_LIMIT + 1):
        chosen = jnp.where(dilation == amount, by_tap, jnp.zeros((), by_tap.dtype))
        for up in range(3):
            blocks += [chosen[3 * up], chosen[3 * up + 2]]
        blocks += [chosen[1], chosen[7]]
    return jnp.concatenate(blocks + [by_tap[4]], axis=0)


def conv_kernel(rows, cols, ext_ref, weight_ref, out_ref, wide_ref, sides_ref):
    limit = DILATION_LIMIT
    wide_ref[...] = ext_ref[...].astype(jnp.float32)
    channels = ext_ref.shape[2]
    for amount in range(1, limit + 1):
        for side, sign in ((0, 1), (1, -1)):
            sides_ref[amount - 1, :, :, side * channels : (side + 1) * channels] = wide_ref[
                :, limit + sign * amount : limit + sign * amount + cols, :
            ].astype(jnp.bfloat16)
    sides_ref[limit, :, :, :channels] = wide_ref[:, limit : limit + cols, :].astype(jnp.bfloat16)

    def one_row(row, carry):
        base = row + limit
        centre = sides_ref[limit, base, :, :channels]
        size = 8 * channels
        total = centre.astype(jnp.float32) + jnp.dot(
            centre, weight_ref[limit * size : limit * size + channels, :], preferred_element_type=jnp.float32
        )
        for amount in range(1, limit + 1):
            at = (amount - 1) * size
            for up in range(3):
                total += jnp.dot(
                    sides_ref[amount - 1, base - amount * (up - 1)],
                    weight_ref[at + 2 * up * channels : at + 2 * (up + 1) * channels, :],
                    preferred_element_type=jnp.float32,
                )
            both = jnp.concatenate(
                [
                    sides_ref[limit, base + amount, :, :channels],
                    sides_ref[limit, base - amount, :, :channels],
                ],
                axis=1,
            )
            total += jnp.dot(
                both, weight_ref[at + 6 * channels : at + 8 * channels, :], preferred_element_type=jnp.float32
            )
        out_ref[row] = total.astype(out_ref.dtype)
        return carry

    lax.fori_loop(0, rows, one_row, 0)


def conv_input_grad(bordered, weights, rows, cols):
    channels = bordered.shape[2]
    tall = bordered.shape[0]
    return pl.pallas_call(
        functools.partial(conv_kernel, rows, cols),
        out_shape=jax.ShapeDtypeStruct((rows, cols, channels), jnp.bfloat16),
        in_specs=[pl.BlockSpec(memory_space=pltpu.VMEM)] * 2,
        out_specs=pl.BlockSpec(memory_space=pltpu.VMEM),
        scratch_shapes=[
            pltpu.VMEM(bordered.shape, jnp.float32),
            pltpu.VMEM((DILATION_LIMIT + 1, tall, cols, 2 * channels), jnp.bfloat16),
        ],
        compiler_params=pltpu.CompilerParams(vmem_limit_bytes=32 * 2**20),
        cost_estimate=pl.CostEstimate(
            flops=2 * 33 * rows * cols * channels * channels, bytes_accessed=3 * 2**20, transcendentals=0
        ),
        name="conv_input_grad",
    )(bordered, weights)


def shift_kernel(rows, cols, ext_ref, dilation_ref, out_ref, wide_ref, picked_ref):
    limit = DILATION_LIMIT
    channels = ext_ref.shape[2]
    wide_ref[...] = ext_ref[...].astype(jnp.float32)
    dilation = dilation_ref[...]

    def columns(row, carry):
        for side in range(3):
            picked = wide_ref[row, limit + side - 1 : limit + side - 1 + cols, :]
            if side != 1:
                for amount in range(2, limit + 1):
                    start = limit + amount * (side - 1)
                    picked = jnp.where(dilation == amount, wide_ref[row, start : start + cols, :], picked)
            picked_ref[side, row] = picked
        return carry

    lax.fori_loop(0, rows + 2 * limit, columns, 0)

    def one_row(row, carry):
        base = row + limit
        start = pl.multiple_of(row * cols, cols)
        for up in range(3):
            for side in range(3):
                picked = picked_ref[side, base + up - 1]
                if up != 1:
                    for amount in range(2, limit + 1):
                        picked = jnp.where(dilation == amount, picked_ref[side, base + amount * (up - 1)], picked)
                tap = 3 * up + side
                out_ref[pl.ds(start, cols), tap * channels : (tap + 1) * channels] = picked.astype(out_ref.dtype)
        return carry

    lax.fori_loop(0, rows, one_row, 0)


def shifted_taps(bordered, dilation, rows, cols):
    channels = bordered.shape[2]
    return pl.pallas_call(
        functools.partial(shift_kernel, rows, cols),
        out_shape=jax.ShapeDtypeStruct((rows * cols, 9 * channels), jnp.bfloat16),
        in_specs=[pl.BlockSpec(memory_space=pltpu.VMEM)] * 2,
        out_specs=pl.BlockSpec(memory_space=pltpu.VMEM),
        scratch_shapes=[
            pltpu.VMEM(bordered.shape, jnp.float32),
            pltpu.VMEM((3, bordered.shape[0], cols, channels), jnp.float32),
        ],
        compiler_params=pltpu.CompilerParams(vmem_limit_bytes=32 * 2**20),
        cost_estimate=pl.CostEstimate(flops=10 * 2**20, bytes_accessed=6 * 2**20, transcendentals=0),
        name="shifted_taps",
    )(bordered, dilation[None, :])


def summed(terms, groups):
    rows, channels = terms.shape
    parts = terms.astype(jnp.bfloat16).reshape(groups, rows // groups, channels)
    parts = lax.all_to_all(parts, "row", split_axis=0, concat_axis=0, tiled=True)
    part = jnp.sum(parts.astype(jnp.float32), axis=0)
    if lax.axis_size("col") > 1:
        part = lax.psum(part, "col")
    spread = jnp.broadcast_to(part[None], (groups,) + part.shape)
    return lax.all_to_all(spread, "row", split_axis=0, concat_axis=0, tiled=True).reshape(rows, channels)


def on_device(
    convolution_input,
    pair,
    out_cot,
    tile_mask,
    dilation,
    norm_in_gain,
    norm_in_bias,
    proj_weight,
    gate_weight,
    norm_out_gain,
    norm_out_bias,
    out_weight,
    out_gate_weight,
    conv_weight,
):
    row_count, col_count, channels = pair.shape
    groups = lax.axis_size("row")
    total_rows = row_count * groups
    share_count = channels // groups
    row_start = lax.axis_index("row") * row_count
    col_start = lax.axis_index("col") * col_count
    tile_count = tile_mask.shape[0]
    tile_size = total_rows // tile_count
    tile_ids = jnp.arange(tile_count, dtype=jnp.int32)
    row_tiles = (row_start + jnp.arange(row_count, dtype=jnp.int32)) // tile_size
    col_tiles = (col_start + jnp.arange(col_count, dtype=jnp.int32)) // tile_size
    row_pick = (row_tiles[:, None] == tile_ids[None, :]).astype(jnp.float32)
    col_pick = (col_tiles[:, None] == tile_ids[None, :]).astype(jnp.float32)
    pair_mask = jnp.dot(jnp.dot(row_pick, tile_mask.astype(jnp.float32)), col_pick.T)
    in_gain = norm_in_gain[None, None, :]
    normed_in, in_hat, in_inv = layer_norm(
        pair.astype(jnp.float32), in_gain, norm_in_bias[None, None, :], 2
    )
    pair_norm = normed_in.astype(jnp.bfloat16)
    projected = jnp.einsum(
        "rkc,ce->erk", pair_norm, proj_weight, preferred_element_type=jnp.float32
    )
    gate_lin = jnp.einsum("rkc,ce->erk", pair_norm, gate_weight, preferred_element_type=jnp.float32)
    gate_sig = jax.nn.sigmoid(gate_lin)
    both_sides = (projected * gate_sig * pair_mask[None]).astype(jnp.bfloat16)
    split_sides = lax.all_to_all(
        both_sides.reshape(2, groups, share_count, row_count, col_count),
        "row",
        split_axis=1,
        concat_axis=3,
        tiled=True,
    )
    left_side = split_sides[0, 0]
    right_side = split_sides[1, 0]
    full_left, full_right = (
        lax.all_gather(left_side, "col", axis=2, tiled=True),
        lax.all_gather(right_side, "col", axis=2, tiled=True),
    )
    own_right = lax.dynamic_slice_in_dim(full_right, col_start, col_count, 1)
    product_split = jnp.einsum(
        "cik,cjk->cij", full_left, own_right, preferred_element_type=jnp.float32
    ).astype(jnp.bfloat16)
    product = lax.all_to_all(product_split, "row", split_axis=1, concat_axis=0, tiled=True)
    out_gain = norm_out_gain[:, None, None]
    normed_out, out_hat, out_inv = layer_norm(
        product.astype(jnp.float32), out_gain, norm_out_bias[:, None, None], 0
    )
    product_norm = normed_out.astype(jnp.bfloat16)
    out_lin = jnp.einsum(
        "crk,cd->rkd", product_norm, out_weight, preferred_element_type=jnp.float32
    )
    out_gate = jax.nn.sigmoid(
        jnp.einsum("rkc,cd->rkd", pair_norm, out_gate_weight, preferred_element_type=jnp.float32)
    )
    cotangent = out_cot.astype(jnp.float32)
    grad_lin = (cotangent * out_gate).astype(jnp.bfloat16)
    grad_gate = (cotangent * out_lin * out_gate * (1.0 - out_gate)).astype(jnp.bfloat16)
    grad_norm = jnp.einsum("rkd,cd->crk", grad_lin, out_weight, preferred_element_type=jnp.float32)
    grad_product = norm_back(grad_norm, out_hat, out_inv, out_gain, 0).astype(jnp.bfloat16)
    grad_split = lax.all_to_all(
        grad_product.reshape(groups, share_count, row_count, col_count),
        "row",
        split_axis=0,
        concat_axis=2,
        tiled=True,
    )[0]
    grad_full = lax.all_gather(grad_split, "col", axis=2, tiled=True)
    grad_left = jnp.einsum(
        "cij,cjk->cik", grad_full, right_side, preferred_element_type=jnp.float32
    )
    grad_right = jnp.einsum(
        "cij,cik->cjk", grad_full, left_side, preferred_element_type=jnp.float32
    )
    grad_pieces = jnp.stack([grad_left, grad_right]).astype(jnp.bfloat16)
    grad_back = lax.all_to_all(grad_pieces, "row", split_axis=2, concat_axis=1, tiled=True)
    grad_sides = (
        grad_back.reshape(2 * channels, row_count, col_count).astype(jnp.float32) * pair_mask[None]
    )
    grad_proj = (grad_sides * gate_sig).astype(jnp.bfloat16)
    grad_gatelin = (grad_sides * projected * gate_sig * (1.0 - gate_sig)).astype(jnp.bfloat16)
    grad_in = jnp.einsum("erk,ce->rkc", grad_proj, proj_weight, preferred_element_type=jnp.float32)
    grad_in = grad_in + jnp.einsum(
        "erk,ce->rkc", grad_gatelin, gate_weight, preferred_element_type=jnp.float32
    )
    grad_in = grad_in + jnp.einsum(
        "rkd,cd->rkc", grad_gate, out_gate_weight, preferred_element_type=jnp.float32
    )
    pair_gradient = (cotangent + norm_back(grad_in, in_hat, in_inv, in_gain, 2)).astype(
        jnp.bfloat16
    )
    bordered_input = extended(convolution_input, (("row", 0), ("col", 1)), DILATION_LIMIT)
    bordered_gradient = extended(pair_gradient, (("row", 0), ("col", 1)), DILATION_LIMIT)
    input_grad = conv_input_grad(bordered_gradient, tap_weights(conv_weight, dilation), row_count, col_count)
    shifted_input = shifted_taps(bordered_input, dilation, row_count, col_count)
    weight_terms = lax.dot_general(
        shifted_input,
        pair_gradient.reshape(row_count * col_count, channels),
        (((0,), (0,)), ((), ())),
        preferred_element_type=jnp.float32,
    )
    weight_total = summed(weight_terms, groups)
    return (input_grad, weight_total.reshape(9, channels, channels) / total_rows)


def solution(mesh):
    placed = (
        P("row", "col", None),
        P("row", "col", None),
        P("row", "col", None),
        P(),
        P(),
        P(),
        P(),
        P(),
        P(),
        P(),
        P(),
        P(),
        P(),
        P(),
    )
    return jax.shard_map(
        on_device,
        mesh=mesh,
        in_specs=placed,
        out_specs=(P("row", "col", None), P()),
        check_vma=False,
    )
```

```python
import functools

import jax
import jax.numpy as jnp
from jax import lax
from jax.experimental import pallas as pl
from jax.experimental.pallas import tpu as pltpu
from jax.sharding import PartitionSpec as P

DILATION_LIMIT = 4


EPSILON = 1e-05


def extended(block, sides, width):
    for axis, dim in sides:
        count = lax.axis_size(axis)
        forward = [(i, i + 1) for i in range(count - 1)]
        backward = [(target, source) for source, target in forward]
        low = lax.ppermute(
            lax.slice_in_dim(block, block.shape[dim] - width, None, axis=dim), axis, forward
        )
        high = lax.ppermute(lax.slice_in_dim(block, 0, width, axis=dim), axis, backward)
        block = jnp.concatenate([low, block, high], axis=dim)
    return block


def layer_norm(value_entries, scale_gain, shift_bias, channel_axis):
    mean_value = jnp.mean(value_entries, axis=channel_axis, keepdims=True)
    centred = value_entries - mean_value
    variance = jnp.mean(centred * centred, axis=channel_axis, keepdims=True)
    inv_deviation = lax.rsqrt(variance + EPSILON)
    normed = centred * inv_deviation
    return (normed * scale_gain + shift_bias, normed, inv_deviation)


def norm_back(incoming, normed, inv_deviation, scale_gain, channel_axis):
    scaled = incoming * scale_gain
    mean_first = jnp.mean(scaled, axis=channel_axis, keepdims=True)
    second = jnp.mean(scaled * normed, axis=channel_axis, keepdims=True)
    return inv_deviation * (scaled - mean_first - normed * second)


def offsets():
    return [
        (row_stride, column_stride) for row_stride in (-1, 0, 1) for column_stride in (-1, 0, 1)
    ]


def greet(groups):
    me = lax.axis_index("row")
    barrier = pltpu.get_barrier_semaphore()

    def one(step, carry):
        peer = lax.rem(me + step, groups)
        pl.semaphore_signal(barrier, inc=1, device_id={"row": peer}, device_id_type=pl.DeviceIdType.MESH)
        return carry

    lax.fori_loop(1, groups, one, 0)
    pl.semaphore_wait(barrier, groups - 1)
    return me


def piece(me, source_ref, landed_ref, send_sem, recv_sem, peer):
    return pltpu.make_async_remote_copy(
        src_ref=source_ref.at[peer],
        dst_ref=landed_ref.at[me],
        send_sem=send_sem.at[peer],
        recv_sem=recv_sem.at[me],
        device_id={"row": peer},
        device_id_type=pl.DeviceIdType.MESH,
    )


def send_all(groups, me, source_ref, landed_ref, send_sem, recv_sem):
    def one(step, carry):
        piece(me, source_ref, landed_ref, send_sem, recv_sem, lax.rem(me + step, groups)).start()
        return carry

    lax.fori_loop(1, groups, one, 0)
    landed_ref[me] = source_ref[me]


def wait_all(groups, me, source_ref, landed_ref, send_sem, recv_sem):
    def one(step, carry):
        peer = lax.rem(me + groups - step, groups)
        pltpu.make_async_remote_copy(
            src_ref=source_ref.at[peer],
            dst_ref=landed_ref.at[peer],
            send_sem=send_sem.at[peer],
            recv_sem=recv_sem.at[peer],
            device_id={"row": peer},
            device_id_type=pl.DeviceIdType.MESH,
        ).wait()
        return carry

    lax.fori_loop(1, groups, one, 0)


def product_kernel(groups, share, rows, cols, source_ref, product_ref, sides_ref, landed, staged, *sems):
    me = greet(groups)
    send_all(groups, me, source_ref, landed, sems[0], sems[1])
    wait_all(groups, me, source_ref, landed, sems[0], sems[1])
    total = groups * rows
    for pair in range(share // 2):
        results = []
        for channel in (2 * pair, 2 * pair + 1):
            both = landed[:, channel].astype(jnp.float32)
            left = both[:, :rows].reshape(total, cols).astype(jnp.bfloat16)
            right = both[:, rows:].reshape(total, cols).astype(jnp.bfloat16)
            sides_ref[channel, 0] = left
            sides_ref[channel, 1] = right
            product = lax.dot_general(
                left, right, (((1,), (1,)), ((), ())), preferred_element_type=jnp.float32
            )
            results.append(product.reshape(groups, rows, total))
        staged[:, 2 * pair * rows : 2 * (pair + 1) * rows, :] = jnp.concatenate(results, axis=1).astype(
            jnp.bfloat16
        )
    send_all(groups, me, staged, product_ref, sems[2], sems[3])
    wait_all(groups, me, staged, product_ref, sems[2], sems[3])


def back_kernel(groups, share, rows, cols, source_ref, sides_ref, grads_ref, landed, staged, *sems):
    me = greet(groups)
    send_all(groups, me, source_ref, landed, sems[0], sems[1])
    wait_all(groups, me, source_ref, landed, sems[0], sems[1])
    total = groups * rows
    for pair in range(share // 2):
        both = landed[:, 2 * pair * rows : 2 * (pair + 1) * rows, :].astype(jnp.float32)
        for part in range(2):
            channel = 2 * pair + part
            incoming = both[:, part * rows : (part + 1) * rows].reshape(total, cols).astype(jnp.bfloat16)
            grad_left = jnp.dot(incoming, sides_ref[channel, 1], preferred_element_type=jnp.float32)
            grad_right = lax.dot_general(
                incoming, sides_ref[channel, 0], (((0,), (0,)), ((), ())), preferred_element_type=jnp.float32
            )
            staged[:, channel] = jnp.concatenate(
                [grad_left.reshape(groups, rows, cols), grad_right.reshape(groups, rows, cols)], axis=1
            ).astype(jnp.bfloat16)
    send_all(groups, me, staged, grads_ref, sems[2], sems[3])
    wait_all(groups, me, staged, grads_ref, sems[2], sems[3])


def triangle_product(source):
    groups, share, two_rows, cols = source.shape
    rows = two_rows // 2
    vmem = pl.BlockSpec(memory_space=pltpu.VMEM)
    return pl.pallas_call(
        functools.partial(product_kernel, groups, share, rows, cols),
        out_shape=(
            jax.ShapeDtypeStruct((groups, share * rows, cols), jnp.bfloat16),
            jax.ShapeDtypeStruct((share, 2, groups * rows, cols), jnp.bfloat16),
        ),
        in_specs=[vmem],
        out_specs=(vmem, vmem),
        scratch_shapes=[
            pltpu.VMEM(source.shape, jnp.bfloat16),
            pltpu.VMEM((groups, share * rows, cols), jnp.bfloat16),
        ]
        + [pltpu.SemaphoreType.DMA((groups,))] * 4,
        compiler_params=pltpu.CompilerParams(
            vmem_limit_bytes=32 * 2**20, collective_id=0, has_side_effects=True
        ),
        name="triangle_product",
    )(source)


def triangle_back(source, sides):
    groups, deep, cols = source.shape
    share = sides.shape[0]
    rows = deep // share
    vmem = pl.BlockSpec(memory_space=pltpu.VMEM)
    shape = (groups, share, 2 * rows, cols)
    return pl.pallas_call(
        functools.partial(back_kernel, groups, share, rows, cols),
        out_shape=jax.ShapeDtypeStruct(shape, jnp.bfloat16),
        in_specs=[vmem, vmem],
        out_specs=vmem,
        scratch_shapes=[pltpu.VMEM(source.shape, jnp.bfloat16), pltpu.VMEM(shape, jnp.bfloat16)]
        + [pltpu.SemaphoreType.DMA((groups,))] * 4,
        compiler_params=pltpu.CompilerParams(
            vmem_limit_bytes=32 * 2**20, collective_id=1, has_side_effects=True
        ),
        name="triangle_back",
    )(source, sides)


def interleaved(weight):
    depth, wide = weight.shape
    return jnp.swapaxes(weight.reshape(depth, 2, wide // 2), 1, 2).reshape(depth, wide)


def tap_weights(conv_weight, dilation):
    by_tap = jnp.swapaxes(conv_weight, 1, 2)
    blocks = []
    for amount in range(1, DILATION_LIMIT + 1):
        chosen = jnp.where(dilation == amount, by_tap, jnp.zeros((), by_tap.dtype))
        for up in range(3):
            blocks += [chosen[3 * up], chosen[3 * up + 2]]
        blocks += [chosen[1], chosen[7]]
    return jnp.concatenate(blocks + [by_tap[4]], axis=0)


def conv_kernel(rows, cols, ext_ref, weight_ref, out_ref, wide_ref, sides_ref):
    limit = DILATION_LIMIT
    wide_ref[...] = ext_ref[...].astype(jnp.float32)
    channels = ext_ref.shape[2]
    for amount in range(1, limit + 1):
        for side, sign in ((0, 1), (1, -1)):
            sides_ref[amount - 1, :, :, side * channels : (side + 1) * channels] = wide_ref[
                :, limit + sign * amount : limit + sign * amount + cols, :
            ].astype(jnp.bfloat16)
    sides_ref[limit, :, :, :channels] = wide_ref[:, limit : limit + cols, :].astype(jnp.bfloat16)

    def one_row(row, carry):
        base = row + limit
        centre = sides_ref[limit, base, :, :channels]
        size = 8 * channels
        total = centre.astype(jnp.float32) + jnp.dot(
            centre, weight_ref[limit * size : limit * size + channels, :], preferred_element_type=jnp.float32
        )
        for amount in range(1, limit + 1):
            at = (amount - 1) * size
            for up in range(3):
                total += jnp.dot(
                    sides_ref[amount - 1, base - amount * (up - 1)],
                    weight_ref[at + 2 * up * channels : at + 2 * (up + 1) * channels, :],
                    preferred_element_type=jnp.float32,
                )
            both = jnp.concatenate(
                [
                    sides_ref[limit, base + amount, :, :channels],
                    sides_ref[limit, base - amount, :, :channels],
                ],
                axis=1,
            )
            total += jnp.dot(
                both, weight_ref[at + 6 * channels : at + 8 * channels, :], preferred_element_type=jnp.float32
            )
        out_ref[row] = total.astype(out_ref.dtype)
        return carry

    lax.fori_loop(0, rows, one_row, 0)


def conv_input_grad(bordered, weights, rows, cols):
    channels = bordered.shape[2]
    tall = bordered.shape[0]
    return pl.pallas_call(
        functools.partial(conv_kernel, rows, cols),
        out_shape=jax.ShapeDtypeStruct((rows, cols, channels), jnp.bfloat16),
        in_specs=[pl.BlockSpec(memory_space=pltpu.VMEM)] * 2,
        out_specs=pl.BlockSpec(memory_space=pltpu.VMEM),
        scratch_shapes=[
            pltpu.VMEM(bordered.shape, jnp.float32),
            pltpu.VMEM((DILATION_LIMIT + 1, tall, cols, 2 * channels), jnp.bfloat16),
        ],
        compiler_params=pltpu.CompilerParams(vmem_limit_bytes=32 * 2**20),
        cost_estimate=pl.CostEstimate(
            flops=2 * 33 * rows * cols * channels * channels, bytes_accessed=3 * 2**20, transcendentals=0
        ),
        name="conv_input_grad",
    )(bordered, weights)


def shift_kernel(rows, cols, ext_ref, dilation_ref, out_ref, wide_ref, picked_ref):
    limit = DILATION_LIMIT
    channels = ext_ref.shape[2]
    wide_ref[...] = ext_ref[...].astype(jnp.float32)
    dilation = dilation_ref[...]

    def columns(row, carry):
        for side in range(3):
            picked = wide_ref[row, limit + side - 1 : limit + side - 1 + cols, :]
            if side != 1:
                for amount in range(2, limit + 1):
                    start = limit + amount * (side - 1)
                    picked = jnp.where(dilation == amount, wide_ref[row, start : start + cols, :], picked)
            picked_ref[side, row] = picked
        return carry

    lax.fori_loop(0, rows + 2 * limit, columns, 0)

    def one_row(row, carry):
        base = row + limit
        start = pl.multiple_of(row * cols, cols)
        for up in range(3):
            for side in range(3):
                picked = picked_ref[side, base + up - 1]
                if up != 1:
                    for amount in range(2, limit + 1):
                        picked = jnp.where(dilation == amount, picked_ref[side, base + amount * (up - 1)], picked)
                tap = 3 * up + side
                out_ref[pl.ds(start, cols), tap * channels : (tap + 1) * channels] = picked.astype(out_ref.dtype)
        return carry

    lax.fori_loop(0, rows, one_row, 0)


def shifted_taps(bordered, dilation, rows, cols):
    channels = bordered.shape[2]
    return pl.pallas_call(
        functools.partial(shift_kernel, rows, cols),
        out_shape=jax.ShapeDtypeStruct((rows * cols, 9 * channels), jnp.bfloat16),
        in_specs=[pl.BlockSpec(memory_space=pltpu.VMEM)] * 2,
        out_specs=pl.BlockSpec(memory_space=pltpu.VMEM),
        scratch_shapes=[
            pltpu.VMEM(bordered.shape, jnp.float32),
            pltpu.VMEM((3, bordered.shape[0], cols, channels), jnp.float32),
        ],
        compiler_params=pltpu.CompilerParams(vmem_limit_bytes=32 * 2**20),
        cost_estimate=pl.CostEstimate(flops=10 * 2**20, bytes_accessed=6 * 2**20, transcendentals=0),
        name="shifted_taps",
    )(bordered, dilation[None, :])


def summed(terms, groups):
    rows, channels = terms.shape
    parts = terms.astype(jnp.bfloat16).reshape(groups, rows // groups, channels)
    parts = lax.all_to_all(parts, "row", split_axis=0, concat_axis=0, tiled=True)
    part = jnp.sum(parts.astype(jnp.float32), axis=0)
    if lax.axis_size("col") > 1:
        part = lax.psum(part, "col")
    spread = jnp.broadcast_to(part[None], (groups,) + part.shape)
    return lax.all_to_all(spread, "row", split_axis=0, concat_axis=0, tiled=True).reshape(rows, channels)


def on_device(
    convolution_input,
    pair,
    out_cot,
    tile_mask,
    dilation,
    norm_in_gain,
    norm_in_bias,
    proj_weight,
    gate_weight,
    norm_out_gain,
    norm_out_bias,
    out_weight,
    out_gate_weight,
    conv_weight,
):
    row_count, col_count, channels = pair.shape
    groups = lax.axis_size("row")
    total_rows = row_count * groups
    share_count = channels // groups
    row_start = lax.axis_index("row") * row_count
    col_start = lax.axis_index("col") * col_count
    tile_count = tile_mask.shape[0]
    tile_size = total_rows // tile_count
    tile_ids = jnp.arange(tile_count, dtype=jnp.int32)
    row_tiles = (row_start + jnp.arange(row_count, dtype=jnp.int32)) // tile_size
    col_tiles = (col_start + jnp.arange(col_count, dtype=jnp.int32)) // tile_size
    row_pick = (row_tiles[:, None] == tile_ids[None, :]).astype(jnp.float32)
    col_pick = (col_tiles[:, None] == tile_ids[None, :]).astype(jnp.float32)
    pair_mask = jnp.dot(jnp.dot(row_pick, tile_mask.astype(jnp.float32)), col_pick.T)
    whole_cols = lax.axis_size("col") == 1 and row_count % 8 == 0 and share_count % 2 == 0
    if whole_cols:
        proj_weight, gate_weight = interleaved(proj_weight), interleaved(gate_weight)
    in_gain = norm_in_gain[None, None, :]
    normed_in, in_hat, in_inv = layer_norm(
        pair.astype(jnp.float32), in_gain, norm_in_bias[None, None, :], 2
    )
    pair_norm = normed_in.astype(jnp.bfloat16)
    projected = jnp.einsum(
        "rkc,ce->erk", pair_norm, proj_weight, preferred_element_type=jnp.float32
    )
    gate_lin = jnp.einsum("rkc,ce->erk", pair_norm, gate_weight, preferred_element_type=jnp.float32)
    gate_sig = jax.nn.sigmoid(gate_lin)
    both_sides = (projected * gate_sig * pair_mask[None]).astype(jnp.bfloat16)
    if whole_cols:
        product, own_sides = triangle_product(
            both_sides.reshape(groups, share_count, 2 * row_count, col_count)
        )
        product = product.reshape(channels, row_count, col_count)
    else:
        split_sides = lax.all_to_all(
            both_sides.reshape(2, groups, share_count, row_count, col_count),
            "row",
            split_axis=1,
            concat_axis=3,
            tiled=True,
        )
        left_side = split_sides[0, 0]
        right_side = split_sides[1, 0]
        full_left, full_right = (
            lax.all_gather(left_side, "col", axis=2, tiled=True),
            lax.all_gather(right_side, "col", axis=2, tiled=True),
        )
        own_right = lax.dynamic_slice_in_dim(full_right, col_start, col_count, 1)
        product_split = jnp.einsum(
            "cik,cjk->cij", full_left, own_right, preferred_element_type=jnp.float32
        ).astype(jnp.bfloat16)
        product = lax.all_to_all(product_split, "row", split_axis=1, concat_axis=0, tiled=True)
    out_gain = norm_out_gain[:, None, None]
    normed_out, out_hat, out_inv = layer_norm(
        product.astype(jnp.float32), out_gain, norm_out_bias[:, None, None], 0
    )
    product_norm = normed_out.astype(jnp.bfloat16)
    out_lin = jnp.einsum(
        "crk,cd->rkd", product_norm, out_weight, preferred_element_type=jnp.float32
    )
    out_gate = jax.nn.sigmoid(
        jnp.einsum("rkc,cd->rkd", pair_norm, out_gate_weight, preferred_element_type=jnp.float32)
    )
    cotangent = out_cot.astype(jnp.float32)
    grad_lin = (cotangent * out_gate).astype(jnp.bfloat16)
    grad_gate = (cotangent * out_lin * out_gate * (1.0 - out_gate)).astype(jnp.bfloat16)
    grad_norm = jnp.einsum("rkd,cd->crk", grad_lin, out_weight, preferred_element_type=jnp.float32)
    grad_product = norm_back(grad_norm, out_hat, out_inv, out_gain, 0).astype(jnp.bfloat16)
    if whole_cols:
        grad_back = triangle_back(
            grad_product.reshape(groups, share_count * row_count, col_count), own_sides
        )
    else:
        grad_split = lax.all_to_all(
            grad_product.reshape(groups, share_count, row_count, col_count),
            "row",
            split_axis=0,
            concat_axis=2,
            tiled=True,
        )[0]
        grad_full = lax.all_gather(grad_split, "col", axis=2, tiled=True)
        grad_left = jnp.einsum(
            "cij,cjk->cik", grad_full, right_side, preferred_element_type=jnp.float32
        )
        grad_right = jnp.einsum(
            "cij,cik->cjk", grad_full, left_side, preferred_element_type=jnp.float32
        )
        grad_pieces = jnp.stack([grad_left, grad_right]).astype(jnp.bfloat16)
        grad_back = lax.all_to_all(grad_pieces, "row", split_axis=2, concat_axis=1, tiled=True)
    grad_sides = (
        grad_back.reshape(2 * channels, row_count, col_count).astype(jnp.float32) * pair_mask[None]
    )
    grad_proj = (grad_sides * gate_sig).astype(jnp.bfloat16)
    grad_gatelin = (grad_sides * projected * gate_sig * (1.0 - gate_sig)).astype(jnp.bfloat16)
    grad_in = jnp.einsum("erk,ce->rkc", grad_proj, proj_weight, preferred_element_type=jnp.float32)
    grad_in = grad_in + jnp.einsum(
        "erk,ce->rkc", grad_gatelin, gate_weight, preferred_element_type=jnp.float32
    )
    grad_in = grad_in + jnp.einsum(
        "rkd,cd->rkc", grad_gate, out_gate_weight, preferred_element_type=jnp.float32
    )
    pair_gradient = (cotangent + norm_back(grad_in, in_hat, in_inv, in_gain, 2)).astype(
        jnp.bfloat16
    )
    bordered_input = extended(convolution_input, (("row", 0), ("col", 1)), DILATION_LIMIT)
    bordered_gradient = extended(pair_gradient, (("row", 0), ("col", 1)), DILATION_LIMIT)
    input_grad = conv_input_grad(bordered_gradient, tap_weights(conv_weight, dilation), row_count, col_count)
    shifted_input = shifted_taps(bordered_input, dilation, row_count, col_count)
    weight_terms = lax.dot_general(
        shifted_input,
        pair_gradient.reshape(row_count * col_count, channels),
        (((0,), (0,)), ((), ())),
        preferred_element_type=jnp.float32,
    )
    weight_total = summed(weight_terms, groups)
    return (input_grad, weight_total.reshape(9, channels, channels) / total_rows)


def solution(mesh):
    placed = (
        P("row", "col", None),
        P("row", "col", None),
        P("row", "col", None),
        P(),
        P(),
        P(),
        P(),
        P(),
        P(),
        P(),
        P(),
        P(),
        P(),
        P(),
    )
    return jax.shard_map(
        on_device,
        mesh=mesh,
        in_specs=placed,
        out_specs=(P("row", "col", None), P()),
        check_vma=False,
    )
```

```python
import functools

import jax
import jax.numpy as jnp
from jax import lax
from jax.experimental import pallas as pl
from jax.experimental.pallas import tpu as pltpu
from jax.sharding import PartitionSpec as P

DILATION_LIMIT = 4


EPSILON = 1e-05


def extended(block, sides, width):
    for axis, dim in sides:
        count = lax.axis_size(axis)
        forward = [(i, i + 1) for i in range(count - 1)]
        backward = [(target, source) for source, target in forward]
        low = lax.ppermute(
            lax.slice_in_dim(block, block.shape[dim] - width, None, axis=dim), axis, forward
        )
        high = lax.ppermute(lax.slice_in_dim(block, 0, width, axis=dim), axis, backward)
        block = jnp.concatenate([low, block, high], axis=dim)
    return block


def layer_norm(value_entries, scale_gain, shift_bias, channel_axis):
    mean_value = jnp.mean(value_entries, axis=channel_axis, keepdims=True)
    centred = value_entries - mean_value
    variance = jnp.mean(centred * centred, axis=channel_axis, keepdims=True)
    inv_deviation = lax.rsqrt(variance + EPSILON)
    normed = centred * inv_deviation
    return (normed * scale_gain + shift_bias, normed, inv_deviation)


def norm_back(incoming, normed, inv_deviation, scale_gain, channel_axis):
    scaled = incoming * scale_gain
    mean_first = jnp.mean(scaled, axis=channel_axis, keepdims=True)
    second = jnp.mean(scaled * normed, axis=channel_axis, keepdims=True)
    return inv_deviation * (scaled - mean_first - normed * second)


def offsets():
    return [
        (row_stride, column_stride) for row_stride in (-1, 0, 1) for column_stride in (-1, 0, 1)
    ]


def greet(groups):
    me = lax.axis_index("row")
    barrier = pltpu.get_barrier_semaphore()

    def one(step, carry):
        peer = lax.rem(me + step, groups)
        pl.semaphore_signal(barrier, inc=1, device_id={"row": peer}, device_id_type=pl.DeviceIdType.MESH)
        return carry

    lax.fori_loop(1, groups, one, 0)
    pl.semaphore_wait(barrier, groups - 1)
    return me


def piece(me, source_ref, landed_ref, send_sem, recv_sem, peer):
    return pltpu.make_async_remote_copy(
        src_ref=source_ref.at[peer],
        dst_ref=landed_ref.at[me],
        send_sem=send_sem.at[peer],
        recv_sem=recv_sem.at[me],
        device_id={"row": peer},
        device_id_type=pl.DeviceIdType.MESH,
    )


def send_all(groups, me, source_ref, landed_ref, send_sem, recv_sem):
    def one(step, carry):
        piece(me, source_ref, landed_ref, send_sem, recv_sem, lax.rem(me + step, groups)).start()
        return carry

    lax.fori_loop(1, groups, one, 0)
    landed_ref[me] = source_ref[me]


def wait_all(groups, me, source_ref, landed_ref, send_sem, recv_sem):
    def one(step, carry):
        peer = lax.rem(me + groups - step, groups)
        pltpu.make_async_remote_copy(
            src_ref=source_ref.at[peer],
            dst_ref=landed_ref.at[peer],
            send_sem=send_sem.at[peer],
            recv_sem=recv_sem.at[peer],
            device_id={"row": peer},
            device_id_type=pl.DeviceIdType.MESH,
        ).wait()
        return carry

    lax.fori_loop(1, groups, one, 0)


def product_kernel(
    groups, share, rows, cols, source_ref, input_ref, dilation_ref, product_ref, sides_ref, taps_ref,
    landed, staged, edge, wide, picked, *sems
):
    me = greet(groups)
    send_edges(groups, me, input_ref, edge, sems[4], sems[5])
    send_all(groups, me, source_ref, landed, sems[0], sems[1])
    fill_own(rows, cols, input_ref, wide)
    wait_edges(groups, me, input_ref, edge, sems[4], sems[5])
    fill_edges(rows, cols, edge, wide)
    pick_taps(rows, cols, dilation_ref[...], wide, picked, taps_ref)
    wait_all(groups, me, source_ref, landed, sems[0], sems[1])
    total = groups * rows
    for pair in range(share // 2):
        results = []
        for channel in (2 * pair, 2 * pair + 1):
            both = landed[:, channel].astype(jnp.float32)
            left = both[:, :rows].reshape(total, cols).astype(jnp.bfloat16)
            right = both[:, rows:].reshape(total, cols).astype(jnp.bfloat16)
            sides_ref[channel, 0] = left
            sides_ref[channel, 1] = right
            product = lax.dot_general(
                left, right, (((1,), (1,)), ((), ())), preferred_element_type=jnp.float32
            )
            results.append(product.reshape(groups, rows, total))
        staged[:, 2 * pair * rows : 2 * (pair + 1) * rows, :] = jnp.concatenate(results, axis=1).astype(
            jnp.bfloat16
        )
    send_all(groups, me, staged, product_ref, sems[2], sems[3])
    wait_all(groups, me, staged, product_ref, sems[2], sems[3])


def back_kernel(groups, share, rows, cols, source_ref, sides_ref, grads_ref, landed, staged, *sems):
    me = greet(groups)
    send_all(groups, me, source_ref, landed, sems[0], sems[1])
    wait_all(groups, me, source_ref, landed, sems[0], sems[1])
    total = groups * rows
    for pair in range(share // 2):
        both = landed[:, 2 * pair * rows : 2 * (pair + 1) * rows, :].astype(jnp.float32)
        for part in range(2):
            channel = 2 * pair + part
            incoming = both[:, part * rows : (part + 1) * rows].reshape(total, cols).astype(jnp.bfloat16)
            grad_left = jnp.dot(incoming, sides_ref[channel, 1], preferred_element_type=jnp.float32)
            grad_right = lax.dot_general(
                incoming, sides_ref[channel, 0], (((0,), (0,)), ((), ())), preferred_element_type=jnp.float32
            )
            staged[:, channel] = jnp.concatenate(
                [grad_left.reshape(groups, rows, cols), grad_right.reshape(groups, rows, cols)], axis=1
            ).astype(jnp.bfloat16)
    send_all(groups, me, staged, grads_ref, sems[2], sems[3])
    wait_all(groups, me, staged, grads_ref, sems[2], sems[3])


def triangle_product(source, conv_input, dilation):
    groups, share, two_rows, cols = source.shape
    rows = two_rows // 2
    channels = conv_input.shape[2]
    limit = DILATION_LIMIT
    tall = rows + 2 * limit
    vmem = pl.BlockSpec(memory_space=pltpu.VMEM)
    return pl.pallas_call(
        functools.partial(product_kernel, groups, share, rows, cols),
        out_shape=(
            jax.ShapeDtypeStruct((groups, share * rows, cols), jnp.bfloat16),
            jax.ShapeDtypeStruct((share, 2, groups * rows, cols), jnp.bfloat16),
            jax.ShapeDtypeStruct((rows * cols, 9 * channels), jnp.bfloat16),
        ),
        in_specs=[vmem] * 3,
        out_specs=(vmem, vmem, vmem),
        scratch_shapes=[
            pltpu.VMEM(source.shape, jnp.bfloat16),
            pltpu.VMEM((groups, share * rows, cols), jnp.bfloat16),
            pltpu.VMEM((2, limit, cols, channels), jnp.bfloat16),
            pltpu.VMEM((tall, cols + 2 * limit, channels), jnp.float32),
            pltpu.VMEM((3, tall, cols, channels), jnp.float32),
        ]
        + [pltpu.SemaphoreType.DMA((groups,))] * 4
        + [pltpu.SemaphoreType.DMA((2,))] * 2,
        compiler_params=pltpu.CompilerParams(
            vmem_limit_bytes=40 * 2**20, collective_id=0, has_side_effects=True
        ),
        name="triangle_product",
    )(source, conv_input, dilation[None, :])


def triangle_back(source, sides):
    groups, deep, cols = source.shape
    share = sides.shape[0]
    rows = deep // share
    vmem = pl.BlockSpec(memory_space=pltpu.VMEM)
    shape = (groups, share, 2 * rows, cols)
    return pl.pallas_call(
        functools.partial(back_kernel, groups, share, rows, cols),
        out_shape=jax.ShapeDtypeStruct(shape, jnp.bfloat16),
        in_specs=[vmem, vmem],
        out_specs=vmem,
        scratch_shapes=[pltpu.VMEM(source.shape, jnp.bfloat16), pltpu.VMEM(shape, jnp.bfloat16)]
        + [pltpu.SemaphoreType.DMA((groups,))] * 4,
        compiler_params=pltpu.CompilerParams(
            vmem_limit_bytes=32 * 2**20, collective_id=1, has_side_effects=True
        ),
        name="triangle_back",
    )(source, sides)


def interleaved(weight):
    depth, wide = weight.shape
    return jnp.swapaxes(weight.reshape(depth, 2, wide // 2), 1, 2).reshape(depth, wide)


def edge_copies(groups, me, block_ref, edge_ref, send_sem, recv_sem):
    rows = block_ref.shape[0]
    limit = DILATION_LIMIT

    def copy(source, slot, peer):
        return pltpu.make_async_remote_copy(
            src_ref=source,
            dst_ref=edge_ref.at[slot],
            send_sem=send_sem.at[slot],
            recv_sem=recv_sem.at[slot],
            device_id={"row": peer},
            device_id_type=pl.DeviceIdType.MESH,
        )

    before = copy(block_ref.at[pl.ds(0, limit)], 1, lax.rem(me + groups - 1, groups))
    after = copy(block_ref.at[pl.ds(rows - limit, limit)], 0, lax.rem(me + 1, groups))
    return before, after


def send_edges(groups, me, block_ref, edge_ref, send_sem, recv_sem):
    before, after = edge_copies(groups, me, block_ref, edge_ref, send_sem, recv_sem)

    @pl.when(me > 0)
    def _():
        before.start()

    @pl.when(me < groups - 1)
    def _():
        after.start()

    @pl.when(me == 0)
    def _():
        edge_ref[0] = jnp.zeros(edge_ref.shape[1:], edge_ref.dtype)

    @pl.when(me == groups - 1)
    def _():
        edge_ref[1] = jnp.zeros(edge_ref.shape[1:], edge_ref.dtype)


def wait_edges(groups, me, block_ref, edge_ref, send_sem, recv_sem):
    before, after = edge_copies(groups, me, block_ref, edge_ref, send_sem, recv_sem)

    @pl.when(me > 0)
    def _():
        before.wait_send()
        after.wait_recv()

    @pl.when(me < groups - 1)
    def _():
        after.wait_send()
        before.wait_recv()


def fill_own(rows, cols, block_ref, wide_ref):
    limit = DILATION_LIMIT
    tall, _, channels = wide_ref.shape
    margin = jnp.zeros((tall, limit, channels), jnp.float32)
    wide_ref[:, :limit, :] = margin
    wide_ref[:, limit + cols :, :] = margin
    wide_ref[limit : limit + rows, limit : limit + cols, :] = block_ref[...].astype(jnp.float32)


def fill_edges(rows, cols, edge_ref, wide_ref):
    limit = DILATION_LIMIT
    wide_ref[:limit, limit : limit + cols, :] = edge_ref[0].astype(jnp.float32)
    wide_ref[limit + rows :, limit : limit + cols, :] = edge_ref[1].astype(jnp.float32)


def conv_rows(cols, first, last, weight_ref, out_ref, sides_ref):
    limit = DILATION_LIMIT
    channels = out_ref.shape[2]

    def one_row(row, carry):
        base = row + limit
        centre = sides_ref[limit, base, :, :channels]
        size = 8 * channels
        total = centre.astype(jnp.float32) + jnp.dot(
            centre, weight_ref[limit * size : limit * size + channels, :], preferred_element_type=jnp.float32
        )
        for amount in range(1, limit + 1):
            at = (amount - 1) * size
            for up in range(3):
                total += jnp.dot(
                    sides_ref[amount - 1, base - amount * (up - 1)],
                    weight_ref[at + 2 * up * channels : at + 2 * (up + 1) * channels, :],
                    preferred_element_type=jnp.float32,
                )
            both = jnp.concatenate(
                [
                    sides_ref[limit, base + amount, :, :channels],
                    sides_ref[limit, base - amount, :, :channels],
                ],
                axis=1,
            )
            total += jnp.dot(
                both, weight_ref[at + 6 * channels : at + 8 * channels, :], preferred_element_type=jnp.float32
            )
        out_ref[row] = total.astype(out_ref.dtype)
        return carry

    lax.fori_loop(first, last, one_row, 0)


def split_columns(cols, first, last, wide_ref, sides_ref):
    limit = DILATION_LIMIT
    channels = wide_ref.shape[2]
    for amount in range(1, limit + 1):
        for side, sign in ((0, 1), (1, -1)):
            sides_ref[amount - 1, first:last, :, side * channels : (side + 1) * channels] = wide_ref[
                first:last, limit + sign * amount : limit + sign * amount + cols, :
            ].astype(jnp.bfloat16)
    sides_ref[limit, first:last, :, :channels] = wide_ref[first:last, limit : limit + cols, :].astype(
        jnp.bfloat16
    )


def last_kernel(
    groups, rows, cols, grad_ref, terms_ref, weight_ref, out_ref, sum_ref, edge, wide, sides, landed, own, *sems
):
    limit = DILATION_LIMIT
    me = greet(groups)
    send_edges(groups, me, grad_ref, edge, sems[0], sems[1])
    send_all(groups, me, terms_ref, landed, sems[2], sems[3])
    fill_own(rows, cols, grad_ref, wide)
    split_columns(cols, limit, limit + rows, wide, sides)
    wait_edges(groups, me, grad_ref, edge, sems[0], sems[1])
    fill_edges(rows, cols, edge, wide)
    split_columns(cols, 0, limit, wide, sides)
    split_columns(cols, limit + rows, rows + 2 * limit, wide, sides)
    wait_all(groups, me, terms_ref, landed, sems[2], sems[3])

    def add(index, total):
        return total + landed[index].astype(jnp.float32)

    total = lax.fori_loop(0, groups, add, jnp.zeros(landed.shape[1:], jnp.float32))
    own[...] = total.astype(jnp.bfloat16)

    def spread(peer):
        return pltpu.make_async_remote_copy(
            src_ref=own,
            dst_ref=sum_ref.at[me],
            send_sem=sems[4].at[peer],
            recv_sem=sems[5].at[me],
            device_id={"row": peer},
            device_id_type=pl.DeviceIdType.MESH,
        )

    def one(step, carry):
        spread(lax.rem(me + step, groups)).start()
        return carry

    lax.fori_loop(1, groups, one, 0)
    sum_ref[me] = own[...]
    conv_rows(cols, 0, rows, weight_ref, out_ref, sides)

    def finish(step, carry):
        peer = lax.rem(me + groups - step, groups)
        pltpu.make_async_remote_copy(
            src_ref=own,
            dst_ref=sum_ref.at[peer],
            send_sem=sems[4].at[peer],
            recv_sem=sems[5].at[peer],
            device_id={"row": peer},
            device_id_type=pl.DeviceIdType.MESH,
        ).wait()
        return carry

    lax.fori_loop(1, groups, finish, 0)


def conv_and_sum(gradient, terms, weights):
    rows, cols, channels = gradient.shape
    groups = terms.shape[0]
    limit = DILATION_LIMIT
    tall = rows + 2 * limit
    vmem = pl.BlockSpec(memory_space=pltpu.VMEM)
    return pl.pallas_call(
        functools.partial(last_kernel, groups, rows, cols),
        out_shape=(
            jax.ShapeDtypeStruct(gradient.shape, jnp.bfloat16),
            jax.ShapeDtypeStruct(terms.shape, jnp.bfloat16),
        ),
        in_specs=[vmem] * 3,
        out_specs=(vmem, vmem),
        scratch_shapes=[
            pltpu.VMEM((2, limit, cols, channels), jnp.bfloat16),
            pltpu.VMEM((tall, cols + 2 * limit, channels), jnp.float32),
            pltpu.VMEM((limit + 1, tall, cols, 2 * channels), jnp.bfloat16),
            pltpu.VMEM(terms.shape, jnp.bfloat16),
            pltpu.VMEM(terms.shape[1:], jnp.bfloat16),
        ]
        + [pltpu.SemaphoreType.DMA((2,))] * 2
        + [pltpu.SemaphoreType.DMA((groups,))] * 4,
        compiler_params=pltpu.CompilerParams(
            vmem_limit_bytes=40 * 2**20, collective_id=2, has_side_effects=True
        ),
        name="conv_and_sum",
    )(gradient, terms, weights)


def tap_weights(conv_weight, dilation):
    by_tap = jnp.swapaxes(conv_weight, 1, 2)
    blocks = []
    for amount in range(1, DILATION_LIMIT + 1):
        chosen = jnp.where(dilation == amount, by_tap, jnp.zeros((), by_tap.dtype))
        for up in range(3):
            blocks += [chosen[3 * up], chosen[3 * up + 2]]
        blocks += [chosen[1], chosen[7]]
    return jnp.concatenate(blocks + [by_tap[4]], axis=0)


def conv_kernel(rows, cols, ext_ref, weight_ref, out_ref, wide_ref, sides_ref):
    limit = DILATION_LIMIT
    wide_ref[...] = ext_ref[...].astype(jnp.float32)
    channels = ext_ref.shape[2]
    for amount in range(1, limit + 1):
        for side, sign in ((0, 1), (1, -1)):
            sides_ref[amount - 1, :, :, side * channels : (side + 1) * channels] = wide_ref[
                :, limit + sign * amount : limit + sign * amount + cols, :
            ].astype(jnp.bfloat16)
    sides_ref[limit, :, :, :channels] = wide_ref[:, limit : limit + cols, :].astype(jnp.bfloat16)

    conv_rows(cols, 0, rows, weight_ref, out_ref, sides_ref)


def conv_input_grad(bordered, weights, rows, cols):
    channels = bordered.shape[2]
    tall = bordered.shape[0]
    return pl.pallas_call(
        functools.partial(conv_kernel, rows, cols),
        out_shape=jax.ShapeDtypeStruct((rows, cols, channels), jnp.bfloat16),
        in_specs=[pl.BlockSpec(memory_space=pltpu.VMEM)] * 2,
        out_specs=pl.BlockSpec(memory_space=pltpu.VMEM),
        scratch_shapes=[
            pltpu.VMEM(bordered.shape, jnp.float32),
            pltpu.VMEM((DILATION_LIMIT + 1, tall, cols, 2 * channels), jnp.bfloat16),
        ],
        compiler_params=pltpu.CompilerParams(vmem_limit_bytes=32 * 2**20),
        cost_estimate=pl.CostEstimate(
            flops=2 * 33 * rows * cols * channels * channels, bytes_accessed=3 * 2**20, transcendentals=0
        ),
        name="conv_input_grad",
    )(bordered, weights)


def pick_taps(rows, cols, dilation, wide_ref, picked_ref, out_ref):
    limit = DILATION_LIMIT
    channels = wide_ref.shape[2]

    def columns(row, carry):
        for side in range(3):
            picked = wide_ref[row, limit + side - 1 : limit + side - 1 + cols, :]
            if side != 1:
                for amount in range(2, limit + 1):
                    start = limit + amount * (side - 1)
                    picked = jnp.where(dilation == amount, wide_ref[row, start : start + cols, :], picked)
            picked_ref[side, row] = picked
        return carry

    lax.fori_loop(0, rows + 2 * limit, columns, 0)

    def one_row(row, carry):
        base = row + limit
        start = pl.multiple_of(row * cols, cols)
        for up in range(3):
            for side in range(3):
                picked = picked_ref[side, base + up - 1]
                if up != 1:
                    for amount in range(2, limit + 1):
                        picked = jnp.where(dilation == amount, picked_ref[side, base + amount * (up - 1)], picked)
                tap = 3 * up + side
                out_ref[pl.ds(start, cols), tap * channels : (tap + 1) * channels] = picked.astype(out_ref.dtype)
        return carry

    lax.fori_loop(0, rows, one_row, 0)


def shift_kernel(rows, cols, ext_ref, dilation_ref, out_ref, wide_ref, picked_ref):
    wide_ref[...] = ext_ref[...].astype(jnp.float32)
    pick_taps(rows, cols, dilation_ref[...], wide_ref, picked_ref, out_ref)


def shifted_taps(bordered, dilation, rows, cols):
    channels = bordered.shape[2]
    return pl.pallas_call(
        functools.partial(shift_kernel, rows, cols),
        out_shape=jax.ShapeDtypeStruct((rows * cols, 9 * channels), jnp.bfloat16),
        in_specs=[pl.BlockSpec(memory_space=pltpu.VMEM)] * 2,
        out_specs=pl.BlockSpec(memory_space=pltpu.VMEM),
        scratch_shapes=[
            pltpu.VMEM(bordered.shape, jnp.float32),
            pltpu.VMEM((3, bordered.shape[0], cols, channels), jnp.float32),
        ],
        compiler_params=pltpu.CompilerParams(vmem_limit_bytes=32 * 2**20),
        cost_estimate=pl.CostEstimate(flops=10 * 2**20, bytes_accessed=6 * 2**20, transcendentals=0),
        name="shifted_taps",
    )(bordered, dilation[None, :])


def summed(terms, groups):
    rows, channels = terms.shape
    parts = terms.astype(jnp.bfloat16).reshape(groups, rows // groups, channels)
    parts = lax.all_to_all(parts, "row", split_axis=0, concat_axis=0, tiled=True)
    part = jnp.sum(parts.astype(jnp.float32), axis=0)
    if lax.axis_size("col") > 1:
        part = lax.psum(part, "col")
    spread = jnp.broadcast_to(part[None], (groups,) + part.shape)
    return lax.all_to_all(spread, "row", split_axis=0, concat_axis=0, tiled=True).reshape(rows, channels)


def on_device(
    convolution_input,
    pair,
    out_cot,
    tile_mask,
    dilation,
    norm_in_gain,
    norm_in_bias,
    proj_weight,
    gate_weight,
    norm_out_gain,
    norm_out_bias,
    out_weight,
    out_gate_weight,
    conv_weight,
):
    row_count, col_count, channels = pair.shape
    groups = lax.axis_size("row")
    total_rows = row_count * groups
    share_count = channels // groups
    row_start = lax.axis_index("row") * row_count
    col_start = lax.axis_index("col") * col_count
    tile_count = tile_mask.shape[0]
    tile_size = total_rows // tile_count
    tile_ids = jnp.arange(tile_count, dtype=jnp.int32)
    row_tiles = (row_start + jnp.arange(row_count, dtype=jnp.int32)) // tile_size
    col_tiles = (col_start + jnp.arange(col_count, dtype=jnp.int32)) // tile_size
    row_pick = (row_tiles[:, None] == tile_ids[None, :]).astype(jnp.float32)
    col_pick = (col_tiles[:, None] == tile_ids[None, :]).astype(jnp.float32)
    pair_mask = jnp.dot(jnp.dot(row_pick, tile_mask.astype(jnp.float32)), col_pick.T)
    whole_cols = lax.axis_size("col") == 1 and row_count % 8 == 0 and share_count % 2 == 0
    if whole_cols:
        proj_weight, gate_weight = interleaved(proj_weight), interleaved(gate_weight)
    in_gain = norm_in_gain[None, None, :]
    normed_in, in_hat, in_inv = layer_norm(
        pair.astype(jnp.float32), in_gain, norm_in_bias[None, None, :], 2
    )
    pair_norm = normed_in.astype(jnp.bfloat16)
    projected = jnp.einsum(
        "rkc,ce->erk", pair_norm, proj_weight, preferred_element_type=jnp.float32
    )
    gate_lin = jnp.einsum("rkc,ce->erk", pair_norm, gate_weight, preferred_element_type=jnp.float32)
    gate_sig = jax.nn.sigmoid(gate_lin)
    both_sides = (projected * gate_sig * pair_mask[None]).astype(jnp.bfloat16)
    if whole_cols:
        product, own_sides, shifted_input = triangle_product(
            both_sides.reshape(groups, share_count, 2 * row_count, col_count), convolution_input, dilation
        )
        product = product.reshape(channels, row_count, col_count)
    else:
        split_sides = lax.all_to_all(
            both_sides.reshape(2, groups, share_count, row_count, col_count),
            "row",
            split_axis=1,
            concat_axis=3,
            tiled=True,
        )
        left_side = split_sides[0, 0]
        right_side = split_sides[1, 0]
        full_left, full_right = (
            lax.all_gather(left_side, "col", axis=2, tiled=True),
            lax.all_gather(right_side, "col", axis=2, tiled=True),
        )
        own_right = lax.dynamic_slice_in_dim(full_right, col_start, col_count, 1)
        product_split = jnp.einsum(
            "cik,cjk->cij", full_left, own_right, preferred_element_type=jnp.float32
        ).astype(jnp.bfloat16)
        product = lax.all_to_all(product_split, "row", split_axis=1, concat_axis=0, tiled=True)
    out_gain = norm_out_gain[:, None, None]
    normed_out, out_hat, out_inv = layer_norm(
        product.astype(jnp.float32), out_gain, norm_out_bias[:, None, None], 0
    )
    product_norm = normed_out.astype(jnp.bfloat16)
    out_lin = jnp.einsum(
        "crk,cd->rkd", product_norm, out_weight, preferred_element_type=jnp.float32
    )
    out_gate = jax.nn.sigmoid(
        jnp.einsum("rkc,cd->rkd", pair_norm, out_gate_weight, preferred_element_type=jnp.float32)
    )
    cotangent = out_cot.astype(jnp.float32)
    grad_lin = (cotangent * out_gate).astype(jnp.bfloat16)
    grad_gate = (cotangent * out_lin * out_gate * (1.0 - out_gate)).astype(jnp.bfloat16)
    grad_norm = jnp.einsum("rkd,cd->crk", grad_lin, out_weight, preferred_element_type=jnp.float32)
    grad_product = norm_back(grad_norm, out_hat, out_inv, out_gain, 0).astype(jnp.bfloat16)
    if whole_cols:
        grad_back = triangle_back(
            grad_product.reshape(groups, share_count * row_count, col_count), own_sides
        )
    else:
        grad_split = lax.all_to_all(
            grad_product.reshape(groups, share_count, row_count, col_count),
            "row",
            split_axis=0,
            concat_axis=2,
            tiled=True,
        )[0]
        grad_full = lax.all_gather(grad_split, "col", axis=2, tiled=True)
        grad_left = jnp.einsum(
            "cij,cjk->cik", grad_full, right_side, preferred_element_type=jnp.float32
        )
        grad_right = jnp.einsum(
            "cij,cik->cjk", grad_full, left_side, preferred_element_type=jnp.float32
        )
        grad_pieces = jnp.stack([grad_left, grad_right]).astype(jnp.bfloat16)
        grad_back = lax.all_to_all(grad_pieces, "row", split_axis=2, concat_axis=1, tiled=True)
    grad_sides = (
        grad_back.reshape(2 * channels, row_count, col_count).astype(jnp.float32) * pair_mask[None]
    )
    grad_proj = (grad_sides * gate_sig).astype(jnp.bfloat16)
    grad_gatelin = (grad_sides * projected * gate_sig * (1.0 - gate_sig)).astype(jnp.bfloat16)
    grad_in = jnp.einsum("erk,ce->rkc", grad_proj, proj_weight, preferred_element_type=jnp.float32)
    grad_in = grad_in + jnp.einsum(
        "erk,ce->rkc", grad_gatelin, gate_weight, preferred_element_type=jnp.float32
    )
    grad_in = grad_in + jnp.einsum(
        "rkd,cd->rkc", grad_gate, out_gate_weight, preferred_element_type=jnp.float32
    )
    pair_gradient = (cotangent + norm_back(grad_in, in_hat, in_inv, in_gain, 2)).astype(
        jnp.bfloat16
    )
    weights = tap_weights(conv_weight, dilation)
    if not whole_cols:
        bordered_input = extended(convolution_input, (("row", 0), ("col", 1)), DILATION_LIMIT)
        shifted_input = shifted_taps(bordered_input, dilation, row_count, col_count)
    weight_terms = lax.dot_general(
        shifted_input,
        pair_gradient.reshape(row_count * col_count, channels),
        (((0,), (0,)), ((), ())),
        preferred_element_type=jnp.float32,
    )
    if whole_cols:
        part = weight_terms.shape[0] // groups
        terms = weight_terms.astype(jnp.bfloat16).reshape(groups, part, channels)
        terms = jnp.pad(terms, ((0, 0), (0, -part % 16), (0, 0)))
        input_grad, weight_total = conv_and_sum(pair_gradient, terms, weights)
        weight_total = weight_total[:, :part].astype(jnp.float32)
    else:
        bordered_gradient = extended(pair_gradient, (("row", 0), ("col", 1)), DILATION_LIMIT)
        input_grad = conv_input_grad(bordered_gradient, weights, row_count, col_count)
        weight_total = summed(weight_terms, groups)
    return (input_grad, weight_total.reshape(9, channels, channels) / total_rows)


def solution(mesh):
    placed = (
        P("row", "col", None),
        P("row", "col", None),
        P("row", "col", None),
        P(),
        P(),
        P(),
        P(),
        P(),
        P(),
        P(),
        P(),
        P(),
        P(),
        P(),
    )
    return jax.shard_map(
        on_device,
        mesh=mesh,
        in_specs=placed,
        out_specs=(P("row", "col", None), P()),
        check_vma=False,
    )
```

```python
import functools

import jax
import jax.numpy as jnp
from jax import lax
from jax.experimental import pallas as pl
from jax.experimental.pallas import tpu as pltpu
from jax.sharding import PartitionSpec as P

DILATION_LIMIT = 4


EPSILON = 1e-05


def extended(block, sides, width):
    for axis, dim in sides:
        count = lax.axis_size(axis)
        forward = [(i, i + 1) for i in range(count - 1)]
        backward = [(target, source) for source, target in forward]
        low = lax.ppermute(
            lax.slice_in_dim(block, block.shape[dim] - width, None, axis=dim), axis, forward
        )
        high = lax.ppermute(lax.slice_in_dim(block, 0, width, axis=dim), axis, backward)
        block = jnp.concatenate([low, block, high], axis=dim)
    return block


def layer_norm(value_entries, scale_gain, shift_bias, channel_axis):
    mean_value = jnp.mean(value_entries, axis=channel_axis, keepdims=True)
    centred = value_entries - mean_value
    variance = jnp.mean(centred * centred, axis=channel_axis, keepdims=True)
    inv_deviation = lax.rsqrt(variance + EPSILON)
    normed = centred * inv_deviation
    return (normed * scale_gain + shift_bias, normed, inv_deviation)


def norm_back(incoming, normed, inv_deviation, scale_gain, channel_axis):
    scaled = incoming * scale_gain
    mean_first = jnp.mean(scaled, axis=channel_axis, keepdims=True)
    second = jnp.mean(scaled * normed, axis=channel_axis, keepdims=True)
    return inv_deviation * (scaled - mean_first - normed * second)


def offsets():
    return [
        (row_stride, column_stride) for row_stride in (-1, 0, 1) for column_stride in (-1, 0, 1)
    ]


def greet(groups):
    me = lax.axis_index("row")
    barrier = pltpu.get_barrier_semaphore()

    def one(step, carry):
        peer = lax.rem(me + step, groups)
        pl.semaphore_signal(barrier, inc=1, device_id={"row": peer}, device_id_type=pl.DeviceIdType.MESH)
        return carry

    lax.fori_loop(1, groups, one, 0)
    pl.semaphore_wait(barrier, groups - 1)
    return me


def piece(me, source_ref, landed_ref, send_sem, recv_sem, peer):
    return pltpu.make_async_remote_copy(
        src_ref=source_ref.at[peer],
        dst_ref=landed_ref.at[me],
        send_sem=send_sem.at[peer],
        recv_sem=recv_sem.at[me],
        device_id={"row": peer},
        device_id_type=pl.DeviceIdType.MESH,
    )


def send_all(groups, me, source_ref, landed_ref, send_sem, recv_sem):
    def one(step, carry):
        piece(me, source_ref, landed_ref, send_sem, recv_sem, lax.rem(me + step, groups)).start()
        return carry

    lax.fori_loop(1, groups, one, 0)
    landed_ref[me] = source_ref[me]


def wait_all(groups, me, source_ref, landed_ref, send_sem, recv_sem):
    def one(step, carry):
        peer = lax.rem(me + groups - step, groups)
        pltpu.make_async_remote_copy(
            src_ref=source_ref.at[peer],
            dst_ref=landed_ref.at[peer],
            send_sem=send_sem.at[peer],
            recv_sem=recv_sem.at[peer],
            device_id={"row": peer},
            device_id_type=pl.DeviceIdType.MESH,
        ).wait()
        return carry

    lax.fori_loop(1, groups, one, 0)


def product_kernel(
    groups, share, rows, cols, source_ref, input_ref, dilation_ref, product_ref, sides_ref, taps_ref,
    landed, staged, edge, wide, picked, *sems
):
    me = greet(groups)
    send_edges(groups, me, input_ref, edge, sems[4], sems[5])
    send_all(groups, me, source_ref, landed, sems[0], sems[1])
    fill_own(rows, cols, input_ref, wide)
    wait_edges(groups, me, input_ref, edge, sems[4], sems[5])
    fill_edges(rows, cols, edge, wide)
    pick_taps(rows, cols, dilation_ref[...], wide, picked, taps_ref)
    wait_all(groups, me, source_ref, landed, sems[0], sems[1])
    total = groups * rows
    for pair in range(share // 2):
        results = []
        for channel in (2 * pair, 2 * pair + 1):
            both = landed[:, channel].astype(jnp.float32)
            left = both[:, :rows].reshape(total, cols).astype(jnp.bfloat16)
            right = both[:, rows:].reshape(total, cols).astype(jnp.bfloat16)
            sides_ref[channel, 0] = left
            sides_ref[channel, 1] = right
            product = lax.dot_general(
                left, right, (((1,), (1,)), ((), ())), preferred_element_type=jnp.float32
            )
            results.append(product.reshape(groups, rows, total))
        staged[:, 2 * pair * rows : 2 * (pair + 1) * rows, :] = jnp.concatenate(results, axis=1).astype(
            jnp.bfloat16
        )
    send_all(groups, me, staged, product_ref, sems[2], sems[3])
    wait_all(groups, me, staged, product_ref, sems[2], sems[3])


def back_kernel(groups, share, rows, cols, source_ref, sides_ref, grads_ref, landed, staged, *sems):
    me = greet(groups)
    send_all(groups, me, source_ref, landed, sems[0], sems[1])
    wait_all(groups, me, source_ref, landed, sems[0], sems[1])
    total = groups * rows
    for pair in range(share // 2):
        both = landed[:, 2 * pair * rows : 2 * (pair + 1) * rows, :].astype(jnp.float32)
        for part in range(2):
            channel = 2 * pair + part
            incoming = both[:, part * rows : (part + 1) * rows].reshape(total, cols).astype(jnp.bfloat16)
            grad_left = jnp.dot(incoming, sides_ref[channel, 1], preferred_element_type=jnp.float32)
            grad_right = lax.dot_general(
                incoming, sides_ref[channel, 0], (((0,), (0,)), ((), ())), preferred_element_type=jnp.float32
            )
            staged[:, channel] = jnp.concatenate(
                [grad_left.reshape(groups, rows, cols), grad_right.reshape(groups, rows, cols)], axis=1
            ).astype(jnp.bfloat16)
    send_all(groups, me, staged, grads_ref, sems[2], sems[3])
    wait_all(groups, me, staged, grads_ref, sems[2], sems[3])


def triangle_product(source, conv_input, dilation):
    groups, share, two_rows, cols = source.shape
    rows = two_rows // 2
    channels = conv_input.shape[2]
    limit = DILATION_LIMIT
    tall = rows + 2 * limit
    vmem = pl.BlockSpec(memory_space=pltpu.VMEM)
    return pl.pallas_call(
        functools.partial(product_kernel, groups, share, rows, cols),
        out_shape=(
            jax.ShapeDtypeStruct((groups, share * rows, cols), jnp.bfloat16),
            jax.ShapeDtypeStruct((share, 2, groups * rows, cols), jnp.bfloat16),
            jax.ShapeDtypeStruct((rows * cols, 9 * channels), jnp.bfloat16),
        ),
        in_specs=[vmem] * 3,
        out_specs=(vmem, vmem, vmem),
        scratch_shapes=[
            pltpu.VMEM(source.shape, jnp.bfloat16),
            pltpu.VMEM((groups, share * rows, cols), jnp.bfloat16),
            pltpu.VMEM((2, limit, cols, channels), jnp.bfloat16),
            pltpu.VMEM((tall, cols + 2 * limit, channels), jnp.float32),
            pltpu.VMEM((3, tall, cols, channels), jnp.float32),
        ]
        + [pltpu.SemaphoreType.DMA((groups,))] * 4
        + [pltpu.SemaphoreType.DMA((2,))] * 2,
        compiler_params=pltpu.CompilerParams(
            vmem_limit_bytes=40 * 2**20, collective_id=0, has_side_effects=True
        ),
        name="triangle_product",
    )(source, conv_input, dilation[None, :])


def triangle_back(source, sides):
    groups, deep, cols = source.shape
    share = sides.shape[0]
    rows = deep // share
    vmem = pl.BlockSpec(memory_space=pltpu.VMEM)
    shape = (groups, share, 2 * rows, cols)
    return pl.pallas_call(
        functools.partial(back_kernel, groups, share, rows, cols),
        out_shape=jax.ShapeDtypeStruct(shape, jnp.bfloat16),
        in_specs=[vmem, vmem],
        out_specs=vmem,
        scratch_shapes=[pltpu.VMEM(source.shape, jnp.bfloat16), pltpu.VMEM(shape, jnp.bfloat16)]
        + [pltpu.SemaphoreType.DMA((groups,))] * 4,
        compiler_params=pltpu.CompilerParams(
            vmem_limit_bytes=32 * 2**20, collective_id=1, has_side_effects=True
        ),
        name="triangle_back",
    )(source, sides)


def interleaved(weight):
    depth, wide = weight.shape
    return jnp.swapaxes(weight.reshape(depth, 2, wide // 2), 1, 2).reshape(depth, wide)


def edge_copies(groups, me, block_ref, edge_ref, send_sem, recv_sem):
    rows = block_ref.shape[0]
    limit = DILATION_LIMIT

    def copy(source, slot, peer):
        return pltpu.make_async_remote_copy(
            src_ref=source,
            dst_ref=edge_ref.at[slot],
            send_sem=send_sem.at[slot],
            recv_sem=recv_sem.at[slot],
            device_id={"row": peer},
            device_id_type=pl.DeviceIdType.MESH,
        )

    before = copy(block_ref.at[pl.ds(0, limit)], 1, lax.rem(me + groups - 1, groups))
    after = copy(block_ref.at[pl.ds(rows - limit, limit)], 0, lax.rem(me + 1, groups))
    return before, after


def send_edges(groups, me, block_ref, edge_ref, send_sem, recv_sem):
    before, after = edge_copies(groups, me, block_ref, edge_ref, send_sem, recv_sem)

    @pl.when(me > 0)
    def _():
        before.start()

    @pl.when(me < groups - 1)
    def _():
        after.start()

    @pl.when(me == 0)
    def _():
        edge_ref[0] = jnp.zeros(edge_ref.shape[1:], edge_ref.dtype)

    @pl.when(me == groups - 1)
    def _():
        edge_ref[1] = jnp.zeros(edge_ref.shape[1:], edge_ref.dtype)


def wait_edges(groups, me, block_ref, edge_ref, send_sem, recv_sem):
    before, after = edge_copies(groups, me, block_ref, edge_ref, send_sem, recv_sem)

    @pl.when(me > 0)
    def _():
        before.wait_send()
        after.wait_recv()

    @pl.when(me < groups - 1)
    def _():
        after.wait_send()
        before.wait_recv()


def fill_own(rows, cols, block_ref, wide_ref):
    limit = DILATION_LIMIT
    tall, _, channels = wide_ref.shape
    margin = jnp.zeros((tall, limit, channels), jnp.float32)
    wide_ref[:, :limit, :] = margin
    wide_ref[:, limit + cols :, :] = margin
    wide_ref[limit : limit + rows, limit : limit + cols, :] = block_ref[...].astype(jnp.float32)


def fill_edges(rows, cols, edge_ref, wide_ref):
    limit = DILATION_LIMIT
    wide_ref[:limit, limit : limit + cols, :] = edge_ref[0].astype(jnp.float32)
    wide_ref[limit + rows :, limit : limit + cols, :] = edge_ref[1].astype(jnp.float32)


def conv_rows(cols, first, last, weight_ref, out_ref, sides_ref):
    limit = DILATION_LIMIT
    channels = out_ref.shape[2]

    def one_row(row, carry):
        base = row + limit
        centre = sides_ref[limit, base, :, :channels]
        size = 8 * channels
        total = centre.astype(jnp.float32) + jnp.dot(
            centre, weight_ref[limit * size : limit * size + channels, :], preferred_element_type=jnp.float32
        )
        for amount in range(1, limit + 1):
            at = (amount - 1) * size
            for up in range(3):
                total += jnp.dot(
                    sides_ref[amount - 1, base - amount * (up - 1)],
                    weight_ref[at + 2 * up * channels : at + 2 * (up + 1) * channels, :],
                    preferred_element_type=jnp.float32,
                )
            both = jnp.concatenate(
                [
                    sides_ref[limit, base + amount, :, :channels],
                    sides_ref[limit, base - amount, :, :channels],
                ],
                axis=1,
            )
            total += jnp.dot(
                both, weight_ref[at + 6 * channels : at + 8 * channels, :], preferred_element_type=jnp.float32
            )
        out_ref[row] = total.astype(out_ref.dtype)
        return carry

    lax.fori_loop(first, last, one_row, 0)


def split_columns(cols, first, last, wide_ref, sides_ref):
    limit = DILATION_LIMIT
    channels = wide_ref.shape[2]
    for amount in range(1, limit + 1):
        for side, sign in ((0, 1), (1, -1)):
            sides_ref[amount - 1, first:last, :, side * channels : (side + 1) * channels] = wide_ref[
                first:last, limit + sign * amount : limit + sign * amount + cols, :
            ].astype(jnp.bfloat16)
    sides_ref[limit, first:last, :, :channels] = wide_ref[first:last, limit : limit + cols, :].astype(
        jnp.bfloat16
    )


def last_kernel(
    groups, rows, cols, grad_ref, terms_ref, weight_ref, out_ref, sum_ref, edge, wide, sides, landed, own, *sems
):
    limit = DILATION_LIMIT
    me = greet(groups)
    send_edges(groups, me, grad_ref, edge, sems[0], sems[1])
    count = terms_ref.shape[0]
    place = (me * count + groups - 1) // groups
    is_owner = (place * groups) // count == me

    def term(index, slot, source):
        return pltpu.make_async_remote_copy(
            src_ref=terms_ref.at[index],
            dst_ref=landed.at[source],
            send_sem=sems[2].at[index],
            recv_sem=sems[3].at[slot],
            device_id={"row": (index * groups) // count},
            device_id_type=pl.DeviceIdType.MESH,
        )

    def give(step, carry):
        index = lax.rem(place + step, count)

        @pl.when((index * groups) // count != me)
        def _():
            term(index, me, me).start()

        return carry

    lax.fori_loop(0, count, give, 0)
    fill_own(rows, cols, grad_ref, wide)
    split_columns(cols, limit, limit + rows, wide, sides)
    wait_edges(groups, me, grad_ref, edge, sems[0], sems[1])
    fill_edges(rows, cols, edge, wide)
    split_columns(cols, 0, limit, wide, sides)
    split_columns(cols, limit + rows, rows + 2 * limit, wide, sides)

    def given(index, carry):
        @pl.when((index * groups) // count != me)
        def _():
            term(index, me, me).wait_send()

        return carry

    def spread(peer, slot):
        return pltpu.make_async_remote_copy(
            src_ref=own,
            dst_ref=sum_ref.at[slot],
            send_sem=sems[4].at[peer],
            recv_sem=sems[5].at[slot],
            device_id={"row": peer},
            device_id_type=pl.DeviceIdType.MESH,
        )

    @pl.when(is_owner)
    def _():
        landed[me] = terms_ref[place]

        def arrive(step, carry):
            peer = lax.rem(me + groups - step, groups)
            term(place, peer, peer).wait_recv()
            return carry

        lax.fori_loop(1, groups, arrive, 0)

        def add(index, total):
            return total + landed[index].astype(jnp.float32)

        total = lax.fori_loop(0, groups, add, jnp.zeros(landed.shape[1:], jnp.float32))
        own[...] = total.astype(jnp.bfloat16)

        def one(step, carry):
            spread(lax.rem(me + step, groups), place).start()
            return carry

        lax.fori_loop(1, groups, one, 0)
        sum_ref[place] = own[...]

    conv_rows(cols, 0, rows, weight_ref, out_ref, sides)
    lax.fori_loop(0, count, given, 0)

    @pl.when(is_owner)
    def _():
        def sent(step, carry):
            spread(lax.rem(me + step, groups), place).wait_send()
            return carry

        lax.fori_loop(1, groups, sent, 0)

    def finish(index, carry):
        @pl.when((index * groups) // count != me)
        def _():
            spread(me, index).wait_recv()

        return carry

    lax.fori_loop(0, count, finish, 0)


def conv_and_sum(gradient, terms, weights, groups):
    rows, cols, channels = gradient.shape
    limit = DILATION_LIMIT
    tall = rows + 2 * limit
    vmem = pl.BlockSpec(memory_space=pltpu.VMEM)
    return pl.pallas_call(
        functools.partial(last_kernel, groups, rows, cols),
        out_shape=(
            jax.ShapeDtypeStruct(gradient.shape, jnp.bfloat16),
            jax.ShapeDtypeStruct(terms.shape, jnp.bfloat16),
        ),
        in_specs=[vmem] * 3,
        out_specs=(vmem, vmem),
        scratch_shapes=[
            pltpu.VMEM((2, limit, cols, channels), jnp.bfloat16),
            pltpu.VMEM((tall, cols + 2 * limit, channels), jnp.float32),
            pltpu.VMEM((limit + 1, tall, cols, 2 * channels), jnp.bfloat16),
            pltpu.VMEM((groups,) + terms.shape[1:], jnp.bfloat16),
            pltpu.VMEM(terms.shape[1:], jnp.bfloat16),
        ]
        + [pltpu.SemaphoreType.DMA((2,))] * 2
        + [pltpu.SemaphoreType.DMA((groups,))] * 4,
        compiler_params=pltpu.CompilerParams(
            vmem_limit_bytes=40 * 2**20, collective_id=2, has_side_effects=True
        ),
        name="conv_and_sum",
    )(gradient, terms, weights)


def tap_weights(conv_weight, dilation):
    by_tap = jnp.swapaxes(conv_weight, 1, 2)
    blocks = []
    for amount in range(1, DILATION_LIMIT + 1):
        chosen = jnp.where(dilation == amount, by_tap, jnp.zeros((), by_tap.dtype))
        for up in range(3):
            blocks += [chosen[3 * up], chosen[3 * up + 2]]
        blocks += [chosen[1], chosen[7]]
    return jnp.concatenate(blocks + [by_tap[4]], axis=0)


def conv_kernel(rows, cols, ext_ref, weight_ref, out_ref, wide_ref, sides_ref):
    limit = DILATION_LIMIT
    wide_ref[...] = ext_ref[...].astype(jnp.float32)
    channels = ext_ref.shape[2]
    for amount in range(1, limit + 1):
        for side, sign in ((0, 1), (1, -1)):
            sides_ref[amount - 1, :, :, side * channels : (side + 1) * channels] = wide_ref[
                :, limit + sign * amount : limit + sign * amount + cols, :
            ].astype(jnp.bfloat16)
    sides_ref[limit, :, :, :channels] = wide_ref[:, limit : limit + cols, :].astype(jnp.bfloat16)

    conv_rows(cols, 0, rows, weight_ref, out_ref, sides_ref)


def conv_input_grad(bordered, weights, rows, cols):
    channels = bordered.shape[2]
    tall = bordered.shape[0]
    return pl.pallas_call(
        functools.partial(conv_kernel, rows, cols),
        out_shape=jax.ShapeDtypeStruct((rows, cols, channels), jnp.bfloat16),
        in_specs=[pl.BlockSpec(memory_space=pltpu.VMEM)] * 2,
        out_specs=pl.BlockSpec(memory_space=pltpu.VMEM),
        scratch_shapes=[
            pltpu.VMEM(bordered.shape, jnp.float32),
            pltpu.VMEM((DILATION_LIMIT + 1, tall, cols, 2 * channels), jnp.bfloat16),
        ],
        compiler_params=pltpu.CompilerParams(vmem_limit_bytes=32 * 2**20),
        cost_estimate=pl.CostEstimate(
            flops=2 * 33 * rows * cols * channels * channels, bytes_accessed=3 * 2**20, transcendentals=0
        ),
        name="conv_input_grad",
    )(bordered, weights)


def pick_taps(rows, cols, dilation, wide_ref, picked_ref, out_ref):
    limit = DILATION_LIMIT
    channels = wide_ref.shape[2]

    def columns(row, carry):
        for side in range(3):
            picked = wide_ref[row, limit + side - 1 : limit + side - 1 + cols, :]
            if side != 1:
                for amount in range(2, limit + 1):
                    start = limit + amount * (side - 1)
                    picked = jnp.where(dilation == amount, wide_ref[row, start : start + cols, :], picked)
            picked_ref[side, row] = picked
        return carry

    lax.fori_loop(0, rows + 2 * limit, columns, 0)

    def one_row(row, carry):
        base = row + limit
        start = pl.multiple_of(row * cols, cols)
        for up in range(3):
            for side in range(3):
                picked = picked_ref[side, base + up - 1]
                if up != 1:
                    for amount in range(2, limit + 1):
                        picked = jnp.where(dilation == amount, picked_ref[side, base + amount * (up - 1)], picked)
                tap = 3 * up + side
                out_ref[pl.ds(start, cols), tap * channels : (tap + 1) * channels] = picked.astype(out_ref.dtype)
        return carry

    lax.fori_loop(0, rows, one_row, 0)


def shift_kernel(rows, cols, ext_ref, dilation_ref, out_ref, wide_ref, picked_ref):
    wide_ref[...] = ext_ref[...].astype(jnp.float32)
    pick_taps(rows, cols, dilation_ref[...], wide_ref, picked_ref, out_ref)


def shifted_taps(bordered, dilation, rows, cols):
    channels = bordered.shape[2]
    return pl.pallas_call(
        functools.partial(shift_kernel, rows, cols),
        out_shape=jax.ShapeDtypeStruct((rows * cols, 9 * channels), jnp.bfloat16),
        in_specs=[pl.BlockSpec(memory_space=pltpu.VMEM)] * 2,
        out_specs=pl.BlockSpec(memory_space=pltpu.VMEM),
        scratch_shapes=[
            pltpu.VMEM(bordered.shape, jnp.float32),
            pltpu.VMEM((3, bordered.shape[0], cols, channels), jnp.float32),
        ],
        compiler_params=pltpu.CompilerParams(vmem_limit_bytes=32 * 2**20),
        cost_estimate=pl.CostEstimate(flops=10 * 2**20, bytes_accessed=6 * 2**20, transcendentals=0),
        name="shifted_taps",
    )(bordered, dilation[None, :])


def summed(terms, groups):
    rows, channels = terms.shape
    parts = terms.astype(jnp.bfloat16).reshape(groups, rows // groups, channels)
    parts = lax.all_to_all(parts, "row", split_axis=0, concat_axis=0, tiled=True)
    part = jnp.sum(parts.astype(jnp.float32), axis=0)
    if lax.axis_size("col") > 1:
        part = lax.psum(part, "col")
    spread = jnp.broadcast_to(part[None], (groups,) + part.shape)
    return lax.all_to_all(spread, "row", split_axis=0, concat_axis=0, tiled=True).reshape(rows, channels)


def on_device(
    convolution_input,
    pair,
    out_cot,
    tile_mask,
    dilation,
    norm_in_gain,
    norm_in_bias,
    proj_weight,
    gate_weight,
    norm_out_gain,
    norm_out_bias,
    out_weight,
    out_gate_weight,
    conv_weight,
):
    row_count, col_count, channels = pair.shape
    groups = lax.axis_size("row")
    total_rows = row_count * groups
    share_count = channels // groups
    row_start = lax.axis_index("row") * row_count
    col_start = lax.axis_index("col") * col_count
    tile_count = tile_mask.shape[0]
    tile_size = total_rows // tile_count
    tile_ids = jnp.arange(tile_count, dtype=jnp.int32)
    row_tiles = (row_start + jnp.arange(row_count, dtype=jnp.int32)) // tile_size
    col_tiles = (col_start + jnp.arange(col_count, dtype=jnp.int32)) // tile_size
    row_pick = (row_tiles[:, None] == tile_ids[None, :]).astype(jnp.float32)
    col_pick = (col_tiles[:, None] == tile_ids[None, :]).astype(jnp.float32)
    pair_mask = jnp.dot(jnp.dot(row_pick, tile_mask.astype(jnp.float32)), col_pick.T)
    whole_cols = lax.axis_size("col") == 1 and row_count % 8 == 0 and share_count % 2 == 0
    if whole_cols:
        proj_weight, gate_weight = interleaved(proj_weight), interleaved(gate_weight)
    in_gain = norm_in_gain[None, None, :]
    normed_in, in_hat, in_inv = layer_norm(
        pair.astype(jnp.float32), in_gain, norm_in_bias[None, None, :], 2
    )
    pair_norm = normed_in.astype(jnp.bfloat16)
    projected = jnp.einsum(
        "rkc,ce->erk", pair_norm, proj_weight, preferred_element_type=jnp.float32
    )
    gate_lin = jnp.einsum("rkc,ce->erk", pair_norm, gate_weight, preferred_element_type=jnp.float32)
    gate_sig = jax.nn.sigmoid(gate_lin)
    both_sides = (projected * gate_sig * pair_mask[None]).astype(jnp.bfloat16)
    if whole_cols:
        product, own_sides, shifted_input = triangle_product(
            both_sides.reshape(groups, share_count, 2 * row_count, col_count), convolution_input, dilation
        )
        product = product.reshape(channels, row_count, col_count)
    else:
        split_sides = lax.all_to_all(
            both_sides.reshape(2, groups, share_count, row_count, col_count),
            "row",
            split_axis=1,
            concat_axis=3,
            tiled=True,
        )
        left_side = split_sides[0, 0]
        right_side = split_sides[1, 0]
        full_left, full_right = (
            lax.all_gather(left_side, "col", axis=2, tiled=True),
            lax.all_gather(right_side, "col", axis=2, tiled=True),
        )
        own_right = lax.dynamic_slice_in_dim(full_right, col_start, col_count, 1)
        product_split = jnp.einsum(
            "cik,cjk->cij", full_left, own_right, preferred_element_type=jnp.float32
        ).astype(jnp.bfloat16)
        product = lax.all_to_all(product_split, "row", split_axis=1, concat_axis=0, tiled=True)
    out_gain = norm_out_gain[:, None, None]
    normed_out, out_hat, out_inv = layer_norm(
        product.astype(jnp.float32), out_gain, norm_out_bias[:, None, None], 0
    )
    product_norm = normed_out.astype(jnp.bfloat16)
    out_lin = jnp.einsum(
        "crk,cd->rkd", product_norm, out_weight, preferred_element_type=jnp.float32
    )
    out_gate = jax.nn.sigmoid(
        jnp.einsum("rkc,cd->rkd", pair_norm, out_gate_weight, preferred_element_type=jnp.float32)
    )
    cotangent = out_cot.astype(jnp.float32)
    grad_lin = (cotangent * out_gate).astype(jnp.bfloat16)
    grad_gate = (cotangent * out_lin * out_gate * (1.0 - out_gate)).astype(jnp.bfloat16)
    grad_norm = jnp.einsum("rkd,cd->crk", grad_lin, out_weight, preferred_element_type=jnp.float32)
    grad_product = norm_back(grad_norm, out_hat, out_inv, out_gain, 0).astype(jnp.bfloat16)
    if whole_cols:
        grad_back = triangle_back(
            grad_product.reshape(groups, share_count * row_count, col_count), own_sides
        )
    else:
        grad_split = lax.all_to_all(
            grad_product.reshape(groups, share_count, row_count, col_count),
            "row",
            split_axis=0,
            concat_axis=2,
            tiled=True,
        )[0]
        grad_full = lax.all_gather(grad_split, "col", axis=2, tiled=True)
        grad_left = jnp.einsum(
            "cij,cjk->cik", grad_full, right_side, preferred_element_type=jnp.float32
        )
        grad_right = jnp.einsum(
            "cij,cik->cjk", grad_full, left_side, preferred_element_type=jnp.float32
        )
        grad_pieces = jnp.stack([grad_left, grad_right]).astype(jnp.bfloat16)
        grad_back = lax.all_to_all(grad_pieces, "row", split_axis=2, concat_axis=1, tiled=True)
    grad_sides = (
        grad_back.reshape(2 * channels, row_count, col_count).astype(jnp.float32) * pair_mask[None]
    )
    grad_proj = (grad_sides * gate_sig).astype(jnp.bfloat16)
    grad_gatelin = (grad_sides * projected * gate_sig * (1.0 - gate_sig)).astype(jnp.bfloat16)
    grad_in = jnp.einsum("erk,ce->rkc", grad_proj, proj_weight, preferred_element_type=jnp.float32)
    grad_in = grad_in + jnp.einsum(
        "erk,ce->rkc", grad_gatelin, gate_weight, preferred_element_type=jnp.float32
    )
    grad_in = grad_in + jnp.einsum(
        "rkd,cd->rkc", grad_gate, out_gate_weight, preferred_element_type=jnp.float32
    )
    pair_gradient = (cotangent + norm_back(grad_in, in_hat, in_inv, in_gain, 2)).astype(
        jnp.bfloat16
    )
    weights = tap_weights(conv_weight, dilation)
    if not whole_cols:
        bordered_input = extended(convolution_input, (("row", 0), ("col", 1)), DILATION_LIMIT)
        shifted_input = shifted_taps(bordered_input, dilation, row_count, col_count)
    weight_terms = lax.dot_general(
        shifted_input,
        pair_gradient.reshape(row_count * col_count, channels),
        (((0,), (0,)), ((), ())),
        preferred_element_type=jnp.float32,
    )
    if whole_cols:
        deep = weight_terms.shape[0]
        part = 16 * (-(-deep // (16 * groups)))
        while deep % part:
            part += 16
        terms = weight_terms.astype(jnp.bfloat16).reshape(deep // part, part, channels)
        input_grad, weight_total = conv_and_sum(pair_gradient, terms, weights, groups)
        weight_total = weight_total.astype(jnp.float32)
    else:
        bordered_gradient = extended(pair_gradient, (("row", 0), ("col", 1)), DILATION_LIMIT)
        input_grad = conv_input_grad(bordered_gradient, weights, row_count, col_count)
        weight_total = summed(weight_terms, groups)
    return (input_grad, weight_total.reshape(9, channels, channels) / total_rows)


def solution(mesh):
    placed = (
        P("row", "col", None),
        P("row", "col", None),
        P("row", "col", None),
        P(),
        P(),
        P(),
        P(),
        P(),
        P(),
        P(),
        P(),
        P(),
        P(),
        P(),
    )
    return jax.shard_map(
        on_device,
        mesh=mesh,
        in_specs=placed,
        out_specs=(P("row", "col", None), P()),
        check_vma=False,
    )
```
